128 devices in a mesh: section: 2 (over z_lo), dp: 4 (over x), fsdp: 16 (over z_hi, y, core).
Axes of the slice: x: 4, y: 4, z: 4 (z_hi: 2, z_lo: 2; z = z_hi * 2 + z_lo), core: 2. Of those that a mesh axis runs over, the one named last changes fastest.
Arguments:
- boundary: bfloat16 [2, 2, 64, 128, 1024], P('section', None, ('dp', 'fsdp')), may hold values from -6 to 6
- mixer_gain: bfloat16 [2, 1024], P('section', 'fsdp'), may hold values from 0.25 to 1.75
- query_weight: bfloat16 [2, 1024, 2048], P('section', 'fsdp'), may hold values from -0.1875 to 0.1875
- key_weight: bfloat16 [2, 1024, 1024], P('section', 'fsdp'), may hold values from -0.1875 to 0.1875
- value_weight: bfloat16 [2, 1024, 1024], P('section', 'fsdp'), may hold values from -0.1875 to 0.1875
- output_weight: bfloat16 [2, 2048, 1024], P('section', 'fsdp'), may hold values from -0.5 to 0.5
- query_gain: bfloat16 [2, 128], P('section', 'fsdp'), may hold values from 0.25 to 1.75
- key_gain: bfloat16 [2, 128], P('section', 'fsdp'), may hold values from 0.25 to 1.75
- dense_gain: bfloat16 [2, 1024], P('section', 'fsdp'), may hold values from 0.25 to 1.75
- gate_weight: bfloat16 [2, 1024, 3072], P('section', 'fsdp'), may hold values from -0.1875 to 0.1875
- up_weight: bfloat16 [2, 1024, 3072], P('section', 'fsdp'), may hold values from -0.1875 to 0.1875
- down_weight: bfloat16 [2, 3072, 1024], P('section', 'fsdp'), may hold values from -0.109375 to 0.109375
Outputs:
- endpoints: float32 [2, 2, 64, 128, 1024], P('section', None, ('dp', 'fsdp'))
- mixer_gain_gradient: float32 [2, 1024], P('section', 'fsdp')
- query_weight_gradient: float32 [2, 1024, 2048], P('section', 'fsdp')
- key_weight_gradient: float32 [2, 1024, 1024], P('section', 'fsdp')
- value_weight_gradient: float32 [2, 1024, 1024], P('section', 'fsdp')
- output_weight_gradient: float32 [2, 2048, 1024], P('section', 'fsdp')
- query_gain_gradient: float32 [2, 128], P('section', 'fsdp')
- key_gain_gradient: float32 [2, 128], P('section', 'fsdp')
- dense_gain_gradient: float32 [2, 1024], P('section', 'fsdp')
- gate_weight_gradient: float32 [2, 1024, 3072], P('section', 'fsdp')
- up_weight_gradient: float32 [2, 1024, 3072], P('section', 'fsdp')
- down_weight_gradient: float32 [2, 3072, 1024], P('section', 'fsdp')
The draws below stay inside these ranges and needn't reach their ends.
All inputs are finite; a program needn't handle non-finite values.
Results may differ from the reference program's by a relative error of at most 0.035.
Values may be sent and summed in bfloat16 or wider, within the bound.
No kernel may reach another device: no remote copies, remote signals or barrier semaphores. Data moves between devices by JAX's collectives and lax.ppermute only.
A program may use at most 640 MiB of HBM per device.

```python
import math
import jax
import jax.numpy as jnp
from jax import lax

D = 1024
HQ = 16
HK = 8
HD = 128
FF = 3072
SEQ = 128
MB = 2
BATCH = 64
N_SECTION = 2


def block_scale(rng, shape, pieces, low, top_value):
    factor_of, own = 1.0, jax.random.fold_in(rng, 6)
    for dim, shards_of in pieces:
        heights = jnp.exp(jax.random.uniform(jax.random.fold_in(own, dim), (shards_of,), jnp.float32, low / len(pieces), top_value / len(pieces)))
        factor_of = factor_of * jnp.repeat(heights, shape[dim] // shards_of).reshape([-1 if axis == dim else 1 for axis in range(len(shape))])
    return factor_of


def centred(rng, dims, deviation, reach, shards=(), kind=jnp.bfloat16):
    values = deviation * jax.random.normal(rng, dims, jnp.float32)
    if shards:
        values = values * block_scale(rng, dims, shards, -0.22, 0.18)
    return jnp.clip(values, -reach, reach).astype(kind)


def setup_inputs(seed: int = 0) -> dict:
    key_of = jax.random.split(jax.random.key(seed), 13)
    boundary = centred(key_of[0], (N_SECTION, MB, BATCH, SEQ, D), 1.0, 6.0, ((0, 2), (2, 64)))
    mixer_gain = jnp.clip(1.0 + 0.15 * jax.random.normal(key_of[1], (N_SECTION, D), jnp.float32), 0.25, 1.75).astype(jnp.bfloat16)
    query_weight = centred(key_of[2], (N_SECTION, D, HQ * HD), D ** -0.5, 0.1875, ((0, 2), (1, 16)))
    key_weight = centred(key_of[3], (N_SECTION, D, HK * HD), D ** -0.5, 0.1875, ((0, 2), (1, 16)))
    value_weight = centred(key_of[4], (N_SECTION, D, HK * HD), D ** -0.5, 0.1875, ((0, 2), (1, 16)))
    output_weight = centred(key_of[5], (N_SECTION, HQ * HD, D), (HQ * HD * 8 // SEQ) ** -0.5, 0.5, ((0, 2), (1, 16)))
    query_gain = jnp.clip(1.0 + 0.15 * jax.random.normal(key_of[6], (N_SECTION, HD), jnp.float32), 0.25, 1.75).astype(jnp.bfloat16)
    key_gain = jnp.clip(1.0 + 0.15 * jax.random.normal(key_of[7], (N_SECTION, HD), jnp.float32), 0.25, 1.75).astype(jnp.bfloat16)
    dense_gain = jnp.clip(1.0 + 0.15 * jax.random.normal(key_of[8], (N_SECTION, D), jnp.float32), 0.25, 1.75).astype(jnp.bfloat16)
    gate_weight = centred(key_of[9], (N_SECTION, D, FF), D ** -0.5, 0.1875, ((0, 2), (1, 16)))
    up_weight = centred(key_of[10], (N_SECTION, D, FF), D ** -0.5, 0.1875, ((0, 2), (1, 16)))
    down_weight = centred(key_of[11], (N_SECTION, FF, D), FF ** -0.5, 0.109375, ((0, 2), (1, 16)))
    return dict(boundary=boundary, mixer_gain=mixer_gain, query_weight=query_weight, key_weight=key_weight, value_weight=value_weight, output_weight=output_weight, query_gain=query_gain, key_gain=key_gain, dense_gain=dense_gain, gate_weight=gate_weight, up_weight=up_weight, down_weight=down_weight)


@jax.custom_vjp
def low(v):
    return lax.optimization_barrier(v.astype(jnp.bfloat16)).astype(jnp.float32)

@jax.custom_vjp
def low_back(v):
    return v

def low_keep(v):
    return (low(v), None)

def low_pass(kept, grad):
    return (grad,)

def back_keep(v):
    return (v, None)

def back_low(kept, grad):
    return (low(grad),)
low.defvjp(low_keep, low_pass)
low_back.defvjp(back_keep, back_low)
epsilon = 1e-06
rope_base = 1000000.0
highest = lax.Precision.HIGHEST

def product(left, right):
    return jnp.matmul(left, right, precision=highest)

def rms_norm(values, gain_vector):
    return values * lax.rsqrt(lax.optimization_barrier(jnp.mean(values * values, axis=-1, keepdims=True)) + epsilon) * gain_vector

def rotate_heads(values):
    half_size = HD // 2
    places = jnp.arange(values.shape[-3], dtype=jnp.float32)
    frequencies = rope_base ** (-jnp.arange(half_size, dtype=jnp.float32) * 2.0 / HD)
    angles = places[:, None] * frequencies[None, :]
    cosine_table = jnp.cos(angles)[:, None, :]
    sine_table = jnp.sin(angles)[:, None, :]
    first_half = values[..., :half_size]
    second_half = values[..., half_size:]
    return jnp.concatenate([first_half * cosine_table - second_half * sine_table, second_half * cosine_table + first_half * sine_table], axis=-1)

def residual_block(hidden_in, weights):
    mixer_gain, query_weight, key_weight, value_weight, output_weight, query_gain, key_gain, dense_gain, gate_weight, up_weight, down_weight = weights
    batch_count, length, features = hidden_in.shape
    query_heads = query_weight.shape[1] // HD
    key_heads = key_weight.shape[1] // HD
    group_size = query_heads // key_heads
    mixer_input = low(rms_norm(hidden_in, mixer_gain))
    queries = low_back(product(mixer_input, query_weight)).reshape(batch_count, length, query_heads, HD)
    keys = low_back(product(mixer_input, key_weight)).reshape(batch_count, length, key_heads, HD)
    values = low(low_back(product(mixer_input, value_weight))).reshape(batch_count, length, key_heads, HD)
    queries = low(rotate_heads(rms_norm(queries, query_gain)))
    keys = low(rotate_heads(rms_norm(keys, key_gain)))
    queries = queries.reshape(batch_count, length, key_heads, group_size, HD)
    scores = low_back(jnp.einsum('bqkgd,bskd->bkgqs', queries, keys, precision=highest) * HD ** (-0.5))
    causal = jnp.arange(length)[:, None] >= jnp.arange(length)[None, :]
    scores = jnp.where(causal, scores, -1e+30)
    weights_soft = low(jax.nn.softmax(scores, axis=-1))
    attended = low(low_back(jnp.einsum('bkgqs,bskd->bqkgd', weights_soft, values, precision=highest)))
    attended = attended.reshape(batch_count, length, query_heads * HD)
    after_mixer = hidden_in + low_back(product(attended, output_weight))
    dense_input = low(rms_norm(after_mixer, dense_gain))
    gate_value = low_back(product(dense_input, gate_weight))
    up_value = low_back(product(dense_input, up_weight))
    hidden_units = low(jax.nn.silu(gate_value) * up_value)
    return after_mixer + low_back(product(hidden_units, down_weight))

def reference(boundary, mixer_gain, query_weight, key_weight, value_weight, output_weight, query_gain, key_gain, dense_gain, gate_weight, up_weight, down_weight):
    weights = tuple((member.astype(jnp.float32) for member in (mixer_gain, query_weight, key_weight, value_weight, output_weight, query_gain, key_gain, dense_gain, gate_weight, up_weight, down_weight)))
    sequences = MB * BATCH
    per_group = math.gcd(sequences, max(1, 4096 // SEQ))
    groups = sequences // per_group
    inputs = boundary[0].astype(jnp.float32).reshape(groups, per_group, SEQ, D)
    cotangents = boundary[1].astype(jnp.float32).reshape(groups, per_group, SEQ, D)

    def both_sections(hidden_in, section_weights):
        first_weights = tuple((member[0] for member in section_weights))
        second_weights = tuple((member[1] for member in section_weights))
        middle = low(low_back(residual_block(hidden_in, first_weights)))
        return residual_block(middle, second_weights)

    def accumulate(totals, group_pair):
        group_inputs, group_cotangents = group_pair
        result, pullback = jax.vjp(both_sections, group_inputs, weights)
        input_gradient, weight_gradients = pullback(group_cotangents)
        return (jax.tree.map(jnp.add, totals, weight_gradients), (result, input_gradient))
    starting = tuple((jnp.zeros_like(member) for member in weights))
    totals, (results, input_gradients) = lax.scan(accumulate, starting, (inputs, cotangents))
    endpoints = jnp.stack([input_gradients.reshape(MB, BATCH, SEQ, D), results.reshape(MB, BATCH, SEQ, D)])
    return (endpoints, totals[0], totals[1], totals[2], totals[3], totals[4], totals[5], totals[6], totals[7], totals[8], totals[9], totals[10])
```

```python
import functools

import jax
import jax.numpy as jnp
from jax import lax
from jax.experimental import pallas as pl
from jax.experimental.pallas import tpu as pltpu
from jax.sharding import PartitionSpec as P

epsilon = 1e-06
rope_base = 1000000.0
low = jnp.bfloat16
f32 = jnp.float32
MODEL = 1024
HEAD = 128
ROOT = HEAD ** (-0.5)


def swap_core(value):
    return lax.ppermute(value, "fsdp", [(i, i ^ 1) for i in range(16)])


def swap_z(value):
    return lax.ppermute(value, "fsdp", [(i, i ^ 8) for i in range(16)])


def move_y(value, step):
    pairs = [(i, (i & 8) | ((((i >> 1) + step) & 3) << 1) | (i & 1)) for i in range(16)]
    return lax.ppermute(value, "fsdp", pairs)


def move_x(value, step):
    return lax.ppermute(value, "dp", [(i, (i + step) % 4) for i in range(4)])


def move_section(value, step):
    return lax.ppermute(value, "section", [(0, 1)] if step > 0 else [(1, 0)])


def pick(value, *where):
    start = list(where) + [0] * (value.ndim - len(where))
    size = [1] * len(where) + list(value.shape[len(where) :])
    return lax.dynamic_slice(value, start, size).reshape(value.shape[len(where) :])


def half_of(value, index, axis):
    width = value.shape[axis] // 2
    return lax.dynamic_slice_in_dim(value, index * width, width, axis)


def in_order(own, other, core, axis):
    first = jnp.where(core == 0, own, other)
    second = jnp.where(core == 0, other, own)
    return jnp.concatenate([first, second], axis=axis)


def placing_kernel(counts, rows, offsets, *refs):
    sources, out, sems = refs[: len(counts)], refs[len(counts)], refs[len(counts) + 1]
    copies, k = [], 0
    for source, count in zip(sources, counts):
        for i in range(count):
            at = pl.multiple_of(offsets[k], 16)
            copies.append(pltpu.make_async_copy(source.at[i], out.at[pl.ds(at, rows)], sems.at[k]))
            k += 1
    for copy in copies:
        copy.start()
    for copy in copies:
        copy.wait()


def place(pieces, offsets, total):
    counts = tuple(p.shape[0] for p in pieces)
    rows, width = pieces[0].shape[1:]
    return pl.pallas_call(
        functools.partial(placing_kernel, counts, rows),
        out_shape=jax.ShapeDtypeStruct((total, width), pieces[0].dtype),
        in_specs=[pl.BlockSpec(memory_space=pltpu.SMEM)]
        + [pl.BlockSpec(memory_space=pl.ANY)] * len(pieces),
        out_specs=pl.BlockSpec(memory_space=pl.ANY),
        scratch_shapes=[pltpu.SemaphoreType.DMA((sum(counts),))],
        compiler_params=pltpu.CompilerParams(vmem_limit_bytes=2**20),
        cost_estimate=pl.CostEstimate(
            flops=0, bytes_accessed=4 * total * width, transcendentals=0
        ),
    )(jnp.stack(offsets).astype(jnp.int32), *pieces)


def gather_chip_rows(block, spot, by_x, flip):
    x, z, y = spot
    rows = block.shape[0]
    part = rows // 4 if by_x else rows
    piece = lax.dynamic_slice_in_dim(block, x * part, part, 0) if by_x else block
    across = swap_z(piece)
    pair = jnp.stack([piece, across])
    behind, ahead = move_y(pair, 1), move_y(pair, -1)
    far_own, far_across = move_y(behind[0], 1), move_y(ahead[1], -1)
    origin = [(0, 0), (1, 0), (0, 1), (1, 1), (0, 3), (1, 3), (0, 2), (1, 2)]
    bases = [((z ^ dz ^ flip) * 4 + ((y - dy) & 3)) * rows for dz, dy in origin]
    if not by_x:
        pieces = (pair, behind, ahead, far_own[None], far_across[None])
        return place(pieces, bases, 8 * rows)
    whole = jnp.concatenate([pair, behind, ahead, far_own[None], far_across[None]])
    x_behind, x_ahead = move_x(whole, 1), move_x(whole, -1)
    x_far_a, x_far_b = move_x(x_behind[:4], 1), move_x(x_ahead[4:], -1)
    pieces = (whole, x_behind, x_ahead, x_far_a, x_far_b)
    offsets = []
    for dx, kept in ((0, bases), (1, bases), (3, bases), (2, bases)):
        offsets += [base + ((x - dx) & 3) * part for base in kept]
    return place(pieces, offsets, 8 * rows)


def added(left, right):
    return (left.astype(f32) + right.astype(f32)).astype(low)


def reduce_x(values, x):
    cut = values.shape[1] // 2
    far = pick(values, (x + 2) & 3)
    up, down = move_x(far[:cut], 1), move_x(far[cut:], -1)
    after, before = pick(values, (x + 1) & 3), pick(values, (x - 1) & 3)
    after = jnp.concatenate([added(after[:cut], up), after[cut:]])
    before = jnp.concatenate([before[:cut], added(before[cut:], down)])
    from_behind, from_ahead = move_x(after, 1), move_x(before, -1)
    own = pick(values, x)
    return (own.astype(f32) + from_behind.astype(f32) + from_ahead.astype(f32)).astype(low)


def reduce_chips(values, z, y):
    other = 1 - z
    up = move_y(pick(values, z, (y + 2) & 3), 1)
    down = move_y(pick(values, other, (y + 2) & 3), -1)
    y_after, y_before = (y + 1) & 3, (y - 1) & 3
    after = jnp.stack([added(pick(values, z, y_after), up), pick(values, other, y_after)])
    before = jnp.stack([pick(values, z, y_before), added(pick(values, other, y_before), down)])
    from_behind, from_ahead = move_y(after, 1), move_y(before, -1)

    def total(k, zi):
        own = pick(values, zi, y)
        return (own.astype(f32) + from_behind[k].astype(f32) + from_ahead[k].astype(f32)).astype(low)

    return added(total(0, z), swap_z(total(1, other)))


def scatter_rows(gradient, spot, by_x, flip):
    x, z, y = spot
    z = z ^ flip
    rows, width = gradient.shape[0] // 8, gradient.shape[1]
    part = rows // 4
    if by_x:
        values = gradient.reshape(8, 4, part, width).transpose(1, 0, 2, 3)
        mine = reduce_x(values, x)
        return reduce_chips(mine.reshape(2, 4, part, width), z, y)
    mine = reduce_chips(gradient.reshape(2, 4, rows, width), z, y)
    return reduce_x(mine.reshape(4, part, width), x)


def gather_x(value, x):
    cut = value.shape[0] // 2
    behind, ahead = move_x(value, 1), move_x(value, -1)
    far = jnp.concatenate([move_x(behind[:cut], 1), move_x(ahead[cut:], -1)])
    ring = jnp.stack([value, ahead, far, behind, value, ahead, far, behind])
    return lax.dynamic_slice_in_dim(ring, (4 - x) & 3, 4, 0)


def packed(value):
    return jnp.concatenate([value[:, k : k + 512] for k in range(0, value.shape[1], 512)])


def unpacked(rows, part, width):
    blocks = [rows[:, k * part : (k + 1) * part] for k in range(width // 512)]
    return jnp.concatenate(blocks, axis=2).reshape(4 * part, width)


def finish(values, x, core):
    sizes = [v.shape for v in values]
    together = gather_x(jnp.concatenate([packed(v) for v in values]), x)
    chips, at = [], 0
    for part, width in sizes:
        n = part * width // 512
        chips.append(unpacked(together[:, at : at + n], part, width))
        at += n
    mine = [half_of(chip, core, 0) for chip in chips]
    theirs = [half_of(chip, 1 - core, 0) for chip in chips]
    arrived = swap_core(jnp.concatenate([packed(t) for t in theirs]))
    outs, at = [], 0
    for (part, width), own in zip(sizes, mine):
        n = 2 * part * width // 512
        rows = arrived[at : at + n]
        at += n
        other = jnp.concatenate(
            [rows[k * 2 * part : (k + 1) * 2 * part] for k in range(width // 512)], axis=1
        )
        outs.append((own.astype(f32), other.astype(f32)))
    return outs


def row_scale(values):
    return lax.rsqrt(jnp.mean(values * values, axis=-1, keepdims=True) + epsilon)


def rotation_tables(length):
    half_size = HEAD // 2
    places = jnp.arange(length, dtype=f32)
    frequencies = rope_base ** (-jnp.arange(half_size, dtype=f32) * 2.0 / HEAD)
    angles = places[:, None] * frequencies[None, :]
    return (jnp.cos(angles)[:, None, :], jnp.sin(angles)[:, None, :])


def rotate_heads(values, tables, sign):
    cosine, sine = tables
    first, second = values[..., : HEAD // 2], values[..., HEAD // 2 :]
    sine = sine * sign
    return jnp.concatenate(
        [first * cosine - second * sine, second * cosine + first * sine], axis=-1
    )


def norm_backward(upstream, normed, scaling, gain_vector):
    gain_part = jnp.sum(upstream * normed, axis=tuple(range(upstream.ndim - 1)))
    scaled = upstream * gain_vector
    return (
        scaling * (scaled - normed * jnp.mean(scaled * normed, axis=-1, keepdims=True)),
        gain_part,
    )


def dot(left, right):
    return jnp.dot(left, right, preferred_element_type=f32)


def dot_t(left, right):
    return lax.dot_general(left, right, (((1,), (1,)), ((), ())), preferred_element_type=f32)


def wide(left, pair):
    return jnp.stack([dot(left, w) for w in pair])


def forward(hidden, weights, gains, tables):
    w_qkv, w_out, w_gu, w_down = weights
    mixer_gain, query_gain, key_gain, dense_gain = gains
    tokens = hidden.shape[0]
    seqs = tokens // 128
    scale_one = row_scale(hidden)
    normed_one = hidden * scale_one
    a1 = (normed_one * mixer_gain).astype(low)
    qkv = wide(a1, w_qkv).reshape(2, seqs, 128, 16, HEAD)
    q, k, v = qkv[..., :8, :], qkv[..., 8:12, :], qkv[..., 12:, :].astype(low)
    q_scale, k_scale = row_scale(q), row_scale(k)
    qn, kn = q * q_scale, k * k_scale
    qr = rotate_heads(qn * query_gain, tables, 1.0).astype(low).reshape(2, seqs, 128, 4, 2, HEAD)
    kr = rotate_heads(kn * key_gain, tables, 1.0).astype(low)
    scores = jnp.einsum("hbqkgd,hbskd->hbkgqs", qr, kr, preferred_element_type=f32) * ROOT
    causal = jnp.arange(128)[:, None] >= jnp.arange(128)[None, :]
    p = jax.nn.softmax(jnp.where(causal, scores, -1e30), axis=-1)
    pb = p.astype(low)
    att = jnp.einsum("hbkgqs,hbskd->bqhkgd", pb, v, preferred_element_type=f32)
    att = att.astype(low).reshape(tokens, 2048)
    after = hidden + dot(att, w_out)
    scale_two = row_scale(after)
    normed_two = after * scale_two
    a2 = (normed_two * dense_gain).astype(low)
    gu = wide(a2, w_gu)
    gate, up = gu[..., :1536], gu[..., 1536:]
    z = (jax.nn.silu(gate) * up).astype(low)
    z = jnp.concatenate([z[0], z[1]], axis=-1)
    out = after + dot(z, w_down)
    saved = (
        (scale_one, normed_one, a1, q_scale, qn, k_scale, kn, qr, kr, v, p, pb, att)
        + (scale_two, normed_two, a2, gate, up, z)
    )
    return out, saved


def backward(cotangent, saved, weights, gains, tables):
    w_qkv, w_out, w_gu, w_down = weights
    mixer_gain, query_gain, key_gain, dense_gain = gains
    (scale_one, normed_one, a1, q_scale, qn, k_scale, kn, qr, kr, v, p, pb, att) = saved[:13]
    scale_two, normed_two, a2, gate, up, z = saved[13:]
    tokens = cotangent.shape[0]
    seqs = tokens // 128
    dm = cotangent.astype(low)
    dz = dot_t(dm, w_down)
    dz = jnp.stack([dz[:, :1536], dz[:, 1536:]])
    sig = jax.nn.sigmoid(gate)
    dg = (dz * up * sig * (1.0 + gate * (1.0 - sig))).astype(low)
    du = (dz * (gate * sig)).astype(low)
    dgu = jnp.concatenate([dg, du], axis=-1)
    da2 = dot_t(dgu[0], w_gu[0]) + dot_t(dgu[1], w_gu[1])
    part, dense_gain_grad = norm_backward(da2, normed_two, scale_two, dense_gain)
    dh2 = cotangent + part
    dr = dh2.astype(low)
    datt = dot_t(dr, w_out).astype(low).reshape(seqs, 128, 2, 4, 2, HEAD)
    dp = jnp.einsum("bqhkgd,hbskd->hbkgqs", datt, v, preferred_element_type=f32)
    dv = jnp.einsum("hbkgqs,bqhkgd->hbskd", pb, datt, preferred_element_type=f32).astype(low)
    ds = (p * (dp - jnp.sum(dp * p, axis=-1, keepdims=True))).astype(low)
    dqr = jnp.einsum("hbkgqs,hbskd->hbqkgd", ds, kr, preferred_element_type=f32)
    dqr = dqr.reshape(2, seqs, 128, 8, HEAD) * ROOT
    dkr = jnp.einsum("hbkgqs,hbqkgd->hbskd", ds, qr, preferred_element_type=f32) * ROOT
    dq, q_gain_grad = norm_backward(rotate_heads(dqr, tables, -1.0), qn, q_scale, query_gain)
    dk, k_gain_grad = norm_backward(rotate_heads(dkr, tables, -1.0), kn, k_scale, key_gain)
    dqkv = jnp.concatenate([dq.astype(low), dk.astype(low), dv], axis=3).reshape(2, tokens, 2048)
    da1 = dot_t(dqkv[0], w_qkv[0]) + dot_t(dqkv[1], w_qkv[1])
    part, mixer_gain_grad = norm_backward(da1, normed_one, scale_one, mixer_gain)
    dh = dh2 + part
    return dh, (dm, dgu, dr, dqkv), (mixer_gain_grad, dense_gain_grad, q_gain_grad, k_gain_grad)


def swapped_halves(value):
    cut = value.shape[1] // 2
    return jnp.concatenate([value[:, cut:], value[:, :cut]], axis=1)


def product(left, left_other, right, right_other):
    both_left = jnp.concatenate([left, left_other])
    both_right = jnp.concatenate([right, right_other])
    dims = (((0,), (0,)), ((), ()))
    return lax.dot_general(both_left, both_right, dims, preferred_element_type=f32).astype(low)


def on_device(
    boundary,
    mixer_gain,
    query_weight,
    key_weight,
    value_weight,
    output_weight,
    query_gain,
    key_gain,
    dense_gain,
    gate_weight,
    up_weight,
    down_weight,
):
    first_section = lax.axis_index("section") == 0
    x = lax.axis_index("dp")
    place_at = lax.axis_index("fsdp")
    core, y, z = place_at & 1, (place_at >> 1) & 3, place_at >> 3
    spot = (x, z, y)
    local = boundary[0, :, 0].astype(f32).reshape(256, MODEL)

    tile = jnp.stack(
        [
            mixer_gain[0],
            dense_gain[0],
            jnp.pad(query_gain[0], (0, 56)),
            jnp.pad(key_gain[0], (0, 56)),
        ]
    )
    tiles = lax.all_gather(tile, "fsdp", axis=0, tiled=False).astype(f32)
    gains = (
        tiles[:, 0].reshape(MODEL),
        tiles[:, 2, :8].reshape(HEAD),
        tiles[:, 3, :8].reshape(HEAD),
        tiles[:, 1].reshape(MODEL),
    )

    def column_half(index):
        def cat(*parts):
            return jnp.concatenate([half_of(p[0], index, 1) for p in parts], axis=1)

        return (
            cat(query_weight, key_weight, value_weight),
            cat(output_weight),
            cat(gate_weight, up_weight),
            cat(down_weight),
        )

    kept, sent = column_half(core), column_half(1 - core)
    came = [swap_core(s) for s in sent]
    chips = [in_order(k, c, core, 0) for k, c in zip(kept, came)]
    zero = jnp.zeros_like(z)
    own_qkv = gather_chip_rows(chips[0], spot, False, zero)
    own_gu = gather_chip_rows(chips[2], spot, True, zero)
    own_out = gather_chip_rows(chips[1], spot, False, core)
    own_down = gather_chip_rows(chips[3], spot, True, core)
    w_qkv = (own_qkv, swap_core(own_qkv))
    w_gu = (own_gu, swap_core(own_gu))

    def columns(own):
        other = swap_core(own)
        cut = own.shape[0] // 2
        return in_order(own, jnp.concatenate([other[cut:], other[:cut]]), core, 1)

    w_out, w_down = columns(own_out), columns(own_down)
    weights = (w_qkv, w_out, w_gu, w_down)

    tables = rotation_tables(128)
    early, _ = forward(local, weights, gains, tables)
    arrived = move_section(early.astype(low), 1).astype(f32)
    out, saved = forward(jnp.where(first_section, local, arrived), weights, gains, tables)
    a1, att, a2, z_low = saved[2], saved[12], saved[15], saved[18]
    early_dh, _, _ = backward(local, saved, weights, gains, tables)
    returned = move_section(early_dh.astype(low), -1).astype(f32)
    cotangent = jnp.where(first_section, returned, local)
    dh, (dm, dgu, dr, dqkv), gain_grads = backward(cotangent, saved, weights, gains, tables)
    endpoints = jnp.where(first_section, dh, out).reshape(1, 2, 1, 128, MODEL)

    a1_o, att_o, a2_o, z_o = [swap_core(v) for v in (a1, att, a2, z_low)]
    att_o, z_o = swapped_halves(att_o), swapped_halves(z_o)
    dm_mine, dr_mine = half_of(dm, core, 1), half_of(dr, core, 1)
    g_down = product(z_low, z_o, dm_mine, swap_core(half_of(dm, 1 - core, 1)))
    g_gu = product(a2, a2_o, dgu[0], swap_core(dgu[1]))
    g_out = product(att, att_o, dr_mine, swap_core(half_of(dr, 1 - core, 1)))
    g_qkv = product(a1, a1_o, dqkv[0], swap_core(dqkv[1]))
    s_gu = scatter_rows(g_gu, spot, True, zero)
    s_down = scatter_rows(g_down, spot, False, core)
    s_out = scatter_rows(g_out, spot, False, core)
    s_qkv = scatter_rows(g_qkv, spot, False, zero)
    (gu, down), (out_w, qkv) = finish((s_gu, s_down), x, core), finish((s_out, s_qkv), x, core)

    def both(pair, start, width):
        return in_order(*(p[:, start : start + width] for p in pair), core, 1)[None]

    sums = lax.psum(jnp.concatenate(gain_grads).reshape(18, 128), ("dp", "fsdp")).reshape(-1)

    def gain_rows(start, width):
        return lax.dynamic_slice_in_dim(sums, start + place_at * width, width, 0)[None]

    return (
        endpoints,
        gain_rows(0, 64),
        both(qkv, 0, 1024),
        both(qkv, 1024, 512),
        both(qkv, 1536, 512),
        both(out_w, 0, 512),
        gain_rows(2048, 8),
        gain_rows(2176, 8),
        gain_rows(1024, 64),
        both(gu, 0, 1536),
        both(gu, 1536, 1536),
        both(down, 0, 512),
    )


def solution(mesh):
    placed = (
        P("section", None, ("dp", "fsdp"), None, None),
        P("section", "fsdp"),
        P("section", "fsdp", None),
        P("section", "fsdp", None),
        P("section", "fsdp", None),
        P("section", "fsdp", None),
        P("section", "fsdp"),
        P("section", "fsdp"),
        P("section", "fsdp"),
        P("section", "fsdp", None),
        P("section", "fsdp", None),
        P("section", "fsdp", None),
    )
    return jax.shard_map(
        on_device,
        mesh=mesh,
        in_specs=placed,
        out_specs=(
            P("section", None, ("dp", "fsdp"), None, None),
            P("section", "fsdp"),
            P("section", "fsdp", None),
            P("section", "fsdp", None),
            P("section", "fsdp", None),
            P("section", "fsdp", None),
            P("section", "fsdp"),
            P("section", "fsdp"),
            P("section", "fsdp"),
            P("section", "fsdp", None),
            P("section", "fsdp", None),
            P("section", "fsdp", None),
        ),
        check_vma=False,
    )
```

```python
import functools

import jax
import jax.numpy as jnp
from jax import lax
from jax.experimental import pallas as pl
from jax.experimental.pallas import tpu as pltpu
from jax.sharding import PartitionSpec as P

epsilon = 1e-06
rope_base = 1000000.0
low = jnp.bfloat16
f32 = jnp.float32
MODEL = 1024
HEAD = 128
ROOT = HEAD ** (-0.5)


def after(value, *others):
    return lax.optimization_barrier((value, *others))[0]


def swap_core(value):
    return lax.ppermute(value, "fsdp", [(i, i ^ 1) for i in range(16)])


def swap_z(value):
    return lax.ppermute(value, "fsdp", [(i, i ^ 8) for i in range(16)])


def move_y(value, step):
    pairs = [(i, (i & 8) | ((((i >> 1) + step) & 3) << 1) | (i & 1)) for i in range(16)]
    return lax.ppermute(value, "fsdp", pairs)


def move_x(value, step):
    return lax.ppermute(value, "dp", [(i, (i + step) % 4) for i in range(4)])


def move_section(value, step):
    return lax.ppermute(value, "section", [(0, 1)] if step > 0 else [(1, 0)])


def doubled(value, core, y, z):
    both = in_order(value[None], swap_core(value[None]), core, 0)
    pair = [(i, i ^ 2) for i in range(16)]
    both = in_order(both, lax.ppermute(both, "fsdp", pair), y & 1, 0)
    pair = [(i, i ^ 4) for i in range(16)]
    both = in_order(both, lax.ppermute(both, "fsdp", pair), y >> 1, 0)
    return in_order(both, swap_z(both), z, 0)


def summed(value):
    for step in (1, 2, 4, 8):
        value = value + lax.ppermute(value, "fsdp", [(i, i ^ step) for i in range(16)])
    for step in (1, 2):
        value = value + lax.ppermute(value, "dp", [(i, i ^ step) for i in range(4)])
    return value


def pick(value, *where):
    start = list(where) + [0] * (value.ndim - len(where))
    size = [1] * len(where) + list(value.shape[len(where) :])
    return lax.dynamic_slice(value, start, size).reshape(value.shape[len(where) :])


def half_of(value, index, axis):
    width = value.shape[axis] // 2
    return lax.dynamic_slice_in_dim(value, index * width, width, axis)


def in_order(own, other, core, axis):
    first = jnp.where(core == 0, own, other)
    second = jnp.where(core == 0, other, own)
    return jnp.concatenate([first, second], axis=axis)


def placing_kernel(counts, rows, offsets, *refs):
    sources, out, sems = refs[: len(counts)], refs[len(counts)], refs[len(counts) + 1]
    copies, k = [], 0
    for source, count in zip(sources, counts):
        for i in range(count):
            at = pl.multiple_of(offsets[k], 16)
            copies.append(pltpu.make_async_copy(source.at[i], out.at[pl.ds(at, rows)], sems.at[k]))
            k += 1
    for copy in copies:
        copy.start()
    for copy in copies:
        copy.wait()


def place(pieces, offsets, total):
    counts = tuple(p.shape[0] for p in pieces)
    rows, width = pieces[0].shape[1:]
    return pl.pallas_call(
        functools.partial(placing_kernel, counts, rows),
        out_shape=jax.ShapeDtypeStruct((total, width), pieces[0].dtype),
        in_specs=[pl.BlockSpec(memory_space=pltpu.SMEM)]
        + [pl.BlockSpec(memory_space=pl.ANY)] * len(pieces),
        out_specs=pl.BlockSpec(memory_space=pltpu.VMEM),
        scratch_shapes=[pltpu.SemaphoreType.DMA((sum(counts),))],
        compiler_params=pltpu.CompilerParams(vmem_limit_bytes=16 * 2**20),
        cost_estimate=pl.CostEstimate(
            flops=0, bytes_accessed=4 * total * width, transcendentals=0
        ),
    )(jnp.stack(offsets).astype(jnp.int32), *pieces)


origins = [(0, 0), (1, 0), (0, 1), (1, 1), (0, 3), (1, 3), (0, 2), (1, 2)]


def chip_bases(rows, z, y, flip):
    return [((z ^ dz ^ flip) * 4 + ((y - dy) & 3)) * rows for dz, dy in origins]


def near_y(pair):
    return move_y(pair, 1), move_y(pair, -1)


def far_y(behind, ahead):
    return move_y(behind[0], 1)[None], move_y(ahead[1], -1)[None]


def near_x(whole):
    return move_x(whole, 1), move_x(whole, -1)


def far_x(behind, ahead):
    return move_x(behind[:4], 1), move_x(ahead[4:], -1)


def place_x(pieces, bases, part, x):
    offsets = []
    for dx in (0, 1, 3, 2):
        offsets += [base + ((x - dx) & 3) * part for base in bases]
    return place(pieces, offsets, 32 * part)


def added(left, right):
    return (left.astype(f32) + right.astype(f32)).astype(low)


def reduce_x_first(values, x):
    cut = values.shape[1] // 2
    far = pick(values, (x + 2) & 3)
    return move_x(far[:cut], 1), move_x(far[cut:], -1)


def reduce_x_second(values, x, first):
    cut = values.shape[1] // 2
    up, down = first
    after_it, before = pick(values, (x + 1) & 3), pick(values, (x - 1) & 3)
    after_it = jnp.concatenate([added(after_it[:cut], up), after_it[cut:]])
    before = jnp.concatenate([before[:cut], added(before[cut:], down)])
    return move_x(after_it, 1), move_x(before, -1)


def reduce_x_third(values, x, second):
    own = pick(values, x)
    return (own.astype(f32) + second[0].astype(f32) + second[1].astype(f32)).astype(low)


def reduce_x(values, x):
    return reduce_x_third(values, x, reduce_x_second(values, x, reduce_x_first(values, x)))


def reduce_y_first(values, z, y):
    far = (y + 2) & 3
    return move_y(pick(values, z, far), 1), move_y(pick(values, 1 - z, far), -1)


def reduce_y_second(values, z, y, first):
    up, down = first
    other, y_after, y_before = 1 - z, (y + 1) & 3, (y - 1) & 3
    after_it = jnp.stack([added(pick(values, z, y_after), up), pick(values, other, y_after)])
    before = jnp.stack([pick(values, z, y_before), added(pick(values, other, y_before), down)])
    return move_y(after_it, 1), move_y(before, -1)


def reduce_z(values, z, y, second):
    def total(k, zi):
        own = pick(values, zi, y)
        return (own.astype(f32) + second[0][k].astype(f32) + second[1][k].astype(f32)).astype(low)

    return added(total(0, z), swap_z(total(1, 1 - z)))


def by_chip(gradient):
    return gradient.reshape(2, 4, gradient.shape[0] // 8, gradient.shape[1])


def by_x(gradient):
    part = gradient.shape[0] // 32
    return gradient.reshape(8, 4, part, gradient.shape[1]).transpose(1, 0, 2, 3)


def quarters(value):
    return value.reshape(4, value.shape[0] // 4, value.shape[1])


def gather_x(value, x):
    cut = value.shape[0] // 2
    behind, ahead = move_x(value, 1), move_x(value, -1)
    far = jnp.concatenate([move_x(behind[:cut], 1), move_x(ahead[cut:], -1)])
    ring = jnp.stack([value, ahead, far, behind, value, ahead, far, behind])
    return lax.dynamic_slice_in_dim(ring, (4 - x) & 3, 4, 0)


def packed(value):
    return jnp.concatenate([value[:, k : k + 512] for k in range(0, value.shape[1], 512)])


def unpacked(rows, part, width):
    blocks = [rows[:, k * part : (k + 1) * part] for k in range(width // 512)]
    return jnp.concatenate(blocks, axis=2).reshape(4 * part, width)


def finish(values, x, core):
    sizes = [v.shape for v in values]
    together = gather_x(jnp.concatenate([packed(v) for v in values]), x)
    chips, at = [], 0
    for part, width in sizes:
        n = part * width // 512
        chips.append(unpacked(together[:, at : at + n], part, width))
        at += n
    mine = [half_of(chip, core, 0) for chip in chips]
    theirs = [half_of(chip, 1 - core, 0) for chip in chips]
    arrived = swap_core(jnp.concatenate([packed(t) for t in theirs]))
    outs, at = [], 0
    for (part, width), own in zip(sizes, mine):
        n = 2 * part * width // 512
        rows = arrived[at : at + n]
        at += n
        other = jnp.concatenate(
            [rows[k * 2 * part : (k + 1) * 2 * part] for k in range(width // 512)], axis=1
        )
        outs.append((own.astype(f32), other.astype(f32)))
    return outs


def row_scale(values):
    return lax.rsqrt(jnp.mean(values * values, axis=-1, keepdims=True) + epsilon)


def rotation_tables(length):
    half_size = HEAD // 2
    places = jnp.arange(length, dtype=f32)
    frequencies = rope_base ** (-jnp.arange(half_size, dtype=f32) * 2.0 / HEAD)
    angles = places[:, None] * frequencies[None, :]
    return (jnp.cos(angles)[:, None, :], jnp.sin(angles)[:, None, :])


def rotate_heads(values, tables, sign):
    cosine, sine = tables
    first, second = values[..., : HEAD // 2], values[..., HEAD // 2 :]
    sine = sine * sign
    return jnp.concatenate(
        [first * cosine - second * sine, second * cosine + first * sine], axis=-1
    )


def norm_backward(upstream, normed, scaling, gain_vector):
    gain_part = jnp.sum(upstream * normed, axis=tuple(range(upstream.ndim - 1)))
    scaled = upstream * gain_vector
    return (
        scaling * (scaled - normed * jnp.mean(scaled * normed, axis=-1, keepdims=True)),
        gain_part,
    )


def dot(left, right):
    return jnp.dot(left, right, preferred_element_type=f32)


def dot_t(left, right):
    return lax.dot_general(left, right, (((1,), (1,)), ((), ())), preferred_element_type=f32)


def wide(left, pair):
    return jnp.stack([dot(left, w) for w in pair])


def forward(hidden, weights, gains, tables):
    w_qkv, w_out, w_gu, w_down = weights
    mixer_gain, query_gain, key_gain, dense_gain = gains
    tokens = hidden.shape[0]
    seqs = tokens // 128
    scale_one = row_scale(hidden)
    normed_one = hidden * scale_one
    a1 = (normed_one * mixer_gain).astype(low)
    qkv = wide(a1, w_qkv).reshape(2, seqs, 128, 16, HEAD)
    q, k, v = qkv[..., :8, :], qkv[..., 8:12, :], qkv[..., 12:, :].astype(low)
    q_scale, k_scale = row_scale(q), row_scale(k)
    qn, kn = q * q_scale, k * k_scale
    qr = rotate_heads(qn * query_gain, tables, 1.0).astype(low).reshape(2, seqs, 128, 4, 2, HEAD)
    kr = rotate_heads(kn * key_gain, tables, 1.0).astype(low)
    scores = jnp.einsum("hbqkgd,hbskd->hbkgqs", qr, kr, preferred_element_type=f32) * ROOT
    causal = jnp.arange(128)[:, None] >= jnp.arange(128)[None, :]
    p = jax.nn.softmax(jnp.where(causal, scores, -1e30), axis=-1)
    pb = p.astype(low)
    att = jnp.einsum("hbkgqs,hbskd->bqhkgd", pb, v, preferred_element_type=f32)
    att = att.astype(low).reshape(tokens, 2048)
    after = hidden + dot(att, w_out)
    scale_two = row_scale(after)
    normed_two = after * scale_two
    a2 = (normed_two * dense_gain).astype(low)
    gu = wide(a2, w_gu)
    gate, up = gu[..., :1536], gu[..., 1536:]
    z = (jax.nn.silu(gate) * up).astype(low)
    z = jnp.concatenate([z[0], z[1]], axis=-1)
    out = after + dot(z, w_down)
    saved = (
        (scale_one, normed_one, a1, q_scale, qn, k_scale, kn, qr, kr, v, p, pb, att)
        + (scale_two, normed_two, a2, gate, up, z)
    )
    return out, saved


def backward(cotangent, saved, weights, gains, tables, between=None):
    w_qkv, w_out, w_gu, w_down = weights
    mixer_gain, query_gain, key_gain, dense_gain = gains
    (scale_one, normed_one, a1, q_scale, qn, k_scale, kn, qr, kr, v, p, pb, att) = saved[:13]
    scale_two, normed_two, a2, gate, up, z = saved[13:]
    tokens = cotangent.shape[0]
    seqs = tokens // 128
    dm = cotangent.astype(low)
    dz = dot_t(dm, w_down)
    dz = jnp.stack([dz[:, :1536], dz[:, 1536:]])
    sig = jax.nn.sigmoid(gate)
    dg = (dz * up * sig * (1.0 + gate * (1.0 - sig))).astype(low)
    du = (dz * (gate * sig)).astype(low)
    dgu = jnp.concatenate([dg, du], axis=-1)
    if between is not None:
        dgu = between[0](dm, dgu)
    da2 = dot_t(dgu[0], w_gu[0]) + dot_t(dgu[1], w_gu[1])
    part, dense_gain_grad = norm_backward(da2, normed_two, scale_two, dense_gain)
    dh2 = cotangent + part
    dr = dh2.astype(low)
    if between is not None:
        dr, g_out = between[1](dr)
    datt = dot_t(dr, w_out).astype(low).reshape(seqs, 128, 2, 4, 2, HEAD)
    dp = jnp.einsum("bqhkgd,hbskd->hbkgqs", datt, v, preferred_element_type=f32)
    dv = jnp.einsum("hbkgqs,bqhkgd->hbskd", pb, datt, preferred_element_type=f32).astype(low)
    ds = (p * (dp - jnp.sum(dp * p, axis=-1, keepdims=True))).astype(low)
    dqr = jnp.einsum("hbkgqs,hbskd->hbqkgd", ds, kr, preferred_element_type=f32)
    dqr = dqr.reshape(2, seqs, 128, 8, HEAD) * ROOT
    dkr = jnp.einsum("hbkgqs,hbqkgd->hbskd", ds, qr, preferred_element_type=f32) * ROOT
    dq, q_gain_grad = norm_backward(rotate_heads(dqr, tables, -1.0), qn, q_scale, query_gain)
    dk, k_gain_grad = norm_backward(rotate_heads(dkr, tables, -1.0), kn, k_scale, key_gain)
    dqkv = jnp.concatenate([dq.astype(low), dk.astype(low), dv], axis=3).reshape(2, tokens, 2048)
    if between is not None:
        dqkv = between[2](dqkv, g_out)
    da1 = dot_t(dqkv[0], w_qkv[0]) + dot_t(dqkv[1], w_qkv[1])
    part, mixer_gain_grad = norm_backward(da1, normed_one, scale_one, mixer_gain)
    dh = dh2 + part
    return dh, (mixer_gain_grad, dense_gain_grad, q_gain_grad, k_gain_grad)


def swapped_halves(value):
    cut = value.shape[1] // 2
    return jnp.concatenate([value[:, cut:], value[:, :cut]], axis=1)


def product(left, left_other, right, right_other):
    both_left = jnp.concatenate([left, left_other])
    both_right = jnp.concatenate([right, right_other])
    dims = (((0,), (0,)), ((), ()))
    return lax.dot_general(both_left, both_right, dims, preferred_element_type=f32).astype(low)


def on_device(
    boundary,
    mixer_gain,
    query_weight,
    key_weight,
    value_weight,
    output_weight,
    query_gain,
    key_gain,
    dense_gain,
    gate_weight,
    up_weight,
    down_weight,
):
    first_section = lax.axis_index("section") == 0
    x = lax.axis_index("dp")
    place_at = lax.axis_index("fsdp")
    core, y, z = place_at & 1, (place_at >> 1) & 3, place_at >> 3
    spot = (x, z, y)
    local = boundary[0, :, 0].astype(f32).reshape(256, MODEL)

    tile = jnp.stack(
        [
            mixer_gain[0],
            dense_gain[0],
            jnp.pad(query_gain[0], (0, 56)),
            jnp.pad(key_gain[0], (0, 56)),
        ]
    )
    tiles = doubled(tile, core, y, z).astype(f32)
    gains = (
        tiles[:, 0].reshape(MODEL),
        tiles[:, 2, :8].reshape(HEAD),
        tiles[:, 3, :8].reshape(HEAD),
        tiles[:, 1].reshape(MODEL),
    )

    def column_half(index):
        def cat(*parts):
            return jnp.concatenate([half_of(p[0], index, 1) for p in parts], axis=1)

        return (
            cat(query_weight, key_weight, value_weight),
            cat(output_weight),
            cat(gate_weight, up_weight),
            cat(down_weight),
        )

    kept, sent = column_half(core), column_half(1 - core)
    zero = jnp.zeros_like(z)

    def quarter(chip):
        part = chip.shape[0] // 4
        return lax.dynamic_slice_in_dim(chip, x * part, part, 0)

    with jax.named_scope("ag_gu"):
        gu_0 = quarter(in_order(kept[2], swap_core(sent[2]), core, 0))
        gu_z = swap_z(gu_0)
        gu_pair = jnp.stack([gu_0, gu_z])
        gu_near = near_y(gu_pair)
        gu_far = far_y(*gu_near)
        gu_all = jnp.concatenate([gu_pair, *gu_near, *gu_far])
        gu_x = near_x(gu_all)
    with jax.named_scope("ag_qkv"):
        qkv_0 = in_order(kept[0], swap_core(after(sent[0], gu_0)), core, 0)
        qkv_z = swap_z(after(qkv_0, gu_z))
        qkv_pair = jnp.stack([qkv_0, qkv_z])
        qkv_near = near_y(after(qkv_pair, *gu_far))
    with jax.named_scope("ag_down"):
        down_0 = quarter(in_order(kept[3], swap_core(after(sent[3], gu_0)), core, 0))
        down_z = swap_z(after(down_0, qkv_z))
        down_pair = jnp.stack([down_0, down_z])
        down_near = near_y(after(down_pair, *gu_far))
        down_far = far_y(*down_near)
        down_all = jnp.concatenate([down_pair, *down_near, *down_far])
    with jax.named_scope("ag_qkv"):
        qkv_far = far_y(*qkv_near)
        own_qkv = place((qkv_pair, *qkv_near, *qkv_far), chip_bases(128, z, y, 0), MODEL)
    with jax.named_scope("ag_out"):
        out_0 = in_order(kept[1], swap_core(after(sent[1], gu_0)), core, 0)
        out_z = swap_z(after(out_0, down_z))
        out_pair = jnp.stack([out_0, out_z])
        out_near = near_y(after(out_pair, *qkv_near))
        out_far = far_y(*after(out_near, *qkv_far))
        own_out = place((out_pair, *out_near, *out_far), chip_bases(256, z, y, core), 2048)
    with jax.named_scope("ag_gu"):
        gu_x_far = far_x(*gu_x)
        own_gu = place_x((gu_all, *gu_x, *gu_x_far), chip_bases(128, z, y, 0), 32, x)
    with jax.named_scope("ag_down"):
        down_x = near_x(after(down_all, *gu_x))
        down_x_far = far_x(*down_x)
        own_down = place_x((down_all, *down_x, *down_x_far), chip_bases(384, z, y, core), 96, x)
    w_qkv = (own_qkv, swap_core(own_qkv))
    w_gu = (own_gu, swap_core(own_gu))

    def columns(own):
        other = swap_core(own)
        cut = own.shape[0] // 2
        return in_order(own, jnp.concatenate([other[cut:], other[:cut]]), core, 1)

    w_out, w_down = columns(own_out), columns(own_down)
    weights = (w_qkv, w_out, w_gu, w_down)

    tables = rotation_tables(128)
    with jax.named_scope("f1"):
        early, _ = forward(local, weights, gains, tables)
    arrived = move_section(early.astype(low), 1).astype(f32)
    with jax.named_scope("f2"):
        out, saved = forward(jnp.where(first_section, local, arrived), weights, gains, tables)
    a1, att, a2, z_low = saved[2], saved[12], saved[15], saved[18]
    with jax.named_scope("b1"):
        early_dh, _ = backward(local, saved, weights, gains, tables)
    returned = move_section(early_dh.astype(low), -1).astype(f32)
    cotangent = jnp.where(first_section, returned, local)

    a1_o, att_o, a2_o, z_o = [swap_core(v) for v in (a1, att, a2, z_low)]
    att_o, z_o = swapped_halves(att_o), swapped_halves(z_o)
    cot_mine, cot_theirs = half_of(cotangent, core, 1), half_of(cotangent, 1 - core, 1)
    z_flip = z ^ core
    done = {}

    def after_dgu(dm, dgu):
        with jax.named_scope("g_gu"):
            g_gu = by_x(product(a2, a2_o, dgu[0], swap_core(dgu[1])))
            done["gu"] = (g_gu, reduce_x_first(g_gu, x))
        with jax.named_scope("g_down"):
            dm_o = swap_core(cot_theirs.astype(low))
            g_down = by_chip(product(z_low, z_o, cot_mine.astype(low), dm_o))
            done["down"] = (g_down, reduce_y_first(g_down, z_flip, y))
        return after(dgu, g_gu, g_down)

    def after_dr(dr):
        with jax.named_scope("rs_gu"):
            g_gu, first = done["gu"]
            first = after(first, dr)
            done["gu2"] = reduce_x_second(g_gu, x, first)
        with jax.named_scope("rs_down"):
            g_down, first = done["down"]
            first = after(first, dr)
            done["down2"] = reduce_y_second(g_down, z_flip, y, first)
        with jax.named_scope("g_out"):
            dr_o = swap_core(half_of(dr, 1 - core, 1))
            g_out = by_chip(product(att, att_o, half_of(dr, core, 1), dr_o))
        return after(dr, g_out, *done["gu"][1], *done["down"][1]), g_out

    def after_attention(dqkv, g_out):
        with jax.named_scope("rs_down"):
            second = after(done["down2"], dqkv)
            done["s_down"] = quarters(reduce_z(done["down"][0], z_flip, y, second))
        with jax.named_scope("rs_out"):
            first = reduce_y_first(after(g_out, *second), z_flip, y)
            done["out"] = (g_out, reduce_y_second(g_out, z_flip, y, first))
        with jax.named_scope("rs_gu"):
            second_gu = after(done["gu2"], dqkv)
            mine = by_chip(
                reduce_x_third(done["gu"][0], x, second_gu).reshape(8 * 32, 3072)
            )
            done["gu3"] = (mine, reduce_y_first(mine, z, y))
        with jax.named_scope("g_qkv"):
            g_qkv = by_chip(product(a1, a1_o, dqkv[0], swap_core(dqkv[1])))
            done["qkv"] = (g_qkv, reduce_y_first(after(g_qkv, *done["gu3"][1]), z, y))
        return after(dqkv, g_qkv, *second_gu)

    with jax.named_scope("b2"):
        dh, gain_grads = backward(
            cotangent, saved, weights, gains, tables, (after_dgu, after_dr, after_attention)
        )
    endpoints = jnp.where(first_section, dh, out).reshape(1, 2, 1, 128, MODEL)
    with jax.named_scope("rs_gu"):
        mine, first = done["gu3"]
        gu_y = reduce_y_second(mine, z, y, first)
        s_gu = reduce_z(mine, z, y, gu_y)
    with jax.named_scope("rs_qkv"):
        g_qkv, first = done["qkv"]
        qkv_y = reduce_y_second(g_qkv, z, y, first)
        s_qkv = reduce_x(quarters(reduce_z(g_qkv, z, y, qkv_y)), x)
    with jax.named_scope("rs_down"):
        s_down = reduce_x(done["s_down"], x)
    with jax.named_scope("rs_out"):
        s_out = reduce_x(quarters(reduce_z(done["out"][0], z_flip, y, done["out"][1])), x)
    with jax.named_scope("fin_a"):
        gu, down = finish((s_gu, s_down), x, core)
    with jax.named_scope("fin_b"):
        out_w, qkv = finish((s_out, s_qkv), x, core)

    def both(pair, start, width):
        return in_order(*(p[:, start : start + width] for p in pair), core, 1)[None]

    sums = summed(jnp.concatenate(gain_grads).reshape(18, 128)).reshape(-1)

    def gain_rows(start, width):
        return lax.dynamic_slice_in_dim(sums, start + place_at * width, width, 0)[None]

    return (
        endpoints,
        gain_rows(0, 64),
        both(qkv, 0, 1024),
        both(qkv, 1024, 512),
        both(qkv, 1536, 512),
        both(out_w, 0, 512),
        gain_rows(2048, 8),
        gain_rows(2176, 8),
        gain_rows(1024, 64),
        both(gu, 0, 1536),
        both(gu, 1536, 1536),
        both(down, 0, 512),
    )


def solution(mesh):
    placed = (
        P("section", None, ("dp", "fsdp"), None, None),
        P("section", "fsdp"),
        P("section", "fsdp", None),
        P("section", "fsdp", None),
        P("section", "fsdp", None),
        P("section", "fsdp", None),
        P("section", "fsdp"),
        P("section", "fsdp"),
        P("section", "fsdp"),
        P("section", "fsdp", None),
        P("section", "fsdp", None),
        P("section", "fsdp", None),
    )
    return jax.shard_map(
        on_device,
        mesh=mesh,
        in_specs=placed,
        out_specs=(
            P("section", None, ("dp", "fsdp"), None, None),
            P("section", "fsdp"),
            P("section", "fsdp", None),
            P("section", "fsdp", None),
            P("section", "fsdp", None),
            P("section", "fsdp", None),
            P("section", "fsdp"),
            P("section", "fsdp"),
            P("section", "fsdp"),
            P("section", "fsdp", None),
            P("section", "fsdp", None),
            P("section", "fsdp", None),
        ),
        check_vma=False,
    )
```

```python
import functools

import jax
import jax.numpy as jnp
from jax import lax
from jax.experimental import pallas as pl
from jax.experimental.pallas import tpu as pltpu
from jax.sharding import PartitionSpec as P

epsilon = 1e-06
rope_base = 1000000.0
low = jnp.bfloat16
f32 = jnp.float32
MODEL = 1024
HEAD = 128
ROOT = HEAD ** (-0.5)


def tied(*values):
    return lax.optimization_barrier(values)


def swap_core(value):
    return lax.ppermute(value, "fsdp", [(i, i ^ 1) for i in range(16)])


def swap_z(value):
    return lax.ppermute(value, "fsdp", [(i, i ^ 8) for i in range(16)])


def move_y(value, step):
    pairs = [(i, (i & 8) | ((((i >> 1) + step) & 3) << 1) | (i & 1)) for i in range(16)]
    return lax.ppermute(value, "fsdp", pairs)


def move_x(value, step):
    return lax.ppermute(value, "dp", [(i, (i + step) % 4) for i in range(4)])


def move_section(value, step):
    return lax.ppermute(value, "section", [(0, 1)] if step > 0 else [(1, 0)])


def summed(value):
    for step in (1, 2, 4, 8):
        value = value + lax.ppermute(value, "fsdp", [(i, i ^ step) for i in range(16)])
    for step in (1, 2):
        value = value + lax.ppermute(value, "dp", [(i, i ^ step) for i in range(4)])
    return value


def pick(value, *where):
    start = list(where) + [0] * (value.ndim - len(where))
    size = [1] * len(where) + list(value.shape[len(where) :])
    return lax.dynamic_slice(value, start, size).reshape(value.shape[len(where) :])


def half_of(value, index, axis):
    width = value.shape[axis] // 2
    return lax.dynamic_slice_in_dim(value, index * width, width, axis)


def in_order(own, other, core, axis):
    first = jnp.where(core == 0, own, other)
    second = jnp.where(core == 0, other, own)
    return jnp.concatenate([first, second], axis=axis)


def placing_kernel(moves, sources_count, skipped, offsets, *refs):
    sources, outs, sems = refs[:sources_count], refs[sources_count + skipped : -1], refs[-1]
    copies = []
    for n, (source, index, row, column, rows, width, out) in enumerate(moves):
        block = sources[source].at[index, pl.ds(row, rows), pl.ds(column, width)]
        at = pl.multiple_of(offsets[n], 16)
        copies.append(pltpu.make_async_copy(block, outs[out].at[pl.ds(at, rows)], sems.at[n]))
    for copy in copies:
        copy.start()
    for copy in copies:
        copy.wait()


def place(pieces, moves, offsets, shapes, waits=()):
    return pl.pallas_call(
        functools.partial(placing_kernel, tuple(moves), len(pieces), len(waits)),
        out_shape=[jax.ShapeDtypeStruct(shape, low) for shape in shapes],
        in_specs=[pl.BlockSpec(memory_space=pltpu.SMEM)]
        + [pl.BlockSpec(memory_space=pl.ANY)] * (len(pieces) + len(waits)),
        out_specs=[pl.BlockSpec(memory_space=pltpu.VMEM)] * len(shapes),
        scratch_shapes=[pltpu.SemaphoreType.DMA((len(moves),))],
        compiler_params=pltpu.CompilerParams(vmem_limit_bytes=16 * 2**20),
    )(jnp.stack(offsets).astype(jnp.int32), *pieces, *waits)


def joining_kernel(core_ref, own, other, out, sems):
    rows, width = own.shape
    cut = rows // 2
    mine = pl.multiple_of(core_ref[0] * width, width)
    theirs = pl.multiple_of((1 - core_ref[0]) * width, width)
    upper, lower = pl.ds(0, cut), pl.ds(cut, cut)
    copies = (
        pltpu.make_async_copy(own, out.at[:, pl.ds(mine, width)], sems.at[0]),
        pltpu.make_async_copy(other.at[lower], out.at[upper, pl.ds(theirs, width)], sems.at[1]),
        pltpu.make_async_copy(other.at[upper], out.at[lower, pl.ds(theirs, width)], sems.at[2]),
    )
    for copy in copies:
        copy.start()
    for copy in copies:
        copy.wait()


def joined(own, core):
    rows, width = own.shape
    return pl.pallas_call(
        joining_kernel,
        out_shape=jax.ShapeDtypeStruct((rows, 2 * width), low),
        in_specs=[pl.BlockSpec(memory_space=pltpu.SMEM)] + [pl.BlockSpec(memory_space=pl.ANY)] * 2,
        out_specs=pl.BlockSpec(memory_space=pltpu.VMEM),
        scratch_shapes=[pltpu.SemaphoreType.DMA((3,))],
        compiler_params=pltpu.CompilerParams(vmem_limit_bytes=16 * 2**20),
    )(core.reshape(1).astype(jnp.int32), own, swap_core(own))


origins = [(0, 0), (1, 0), (0, 1), (1, 1), (0, 3), (1, 3), (0, 2), (1, 2)]


def near_y(pair):
    return move_y(pair, 1), move_y(pair, -1)


def far_y(behind, ahead):
    return move_y(behind[0], 1)[None], move_y(ahead[1], -1)[None]


def near_x(whole):
    return move_x(whole, 1), move_x(whole, -1)


def far_x(behind, ahead):
    return move_x(behind[:4], 1), move_x(ahead[4:], -1)


def added(left, right):
    return (left.astype(f32) + right.astype(f32)).astype(low)


def reduce_x_first(take, x):
    far = take((x + 2) & 3)
    cut = far.shape[0] // 2
    return move_x(far[:cut], 1), move_x(far[cut:], -1)


def reduce_x_ready(take, x, first):
    up, down = first
    cut = up.shape[0]
    after_it, before = take((x + 1) & 3), take((x - 1) & 3)
    after_it = jnp.concatenate([added(after_it[:cut], up), after_it[cut:]])
    before = jnp.concatenate([before[:cut], added(before[cut:], down)])
    return after_it, before


def reduce_x_third(take, x, second):
    own = take(x)
    return (own.astype(f32) + second[0].astype(f32) + second[1].astype(f32)).astype(low)


def reduce_x(values, x):
    def take(place):
        return pick(values, place)

    second = near_x_two(*reduce_x_ready(take, x, reduce_x_first(take, x)))
    return reduce_x_third(take, x, second)


def near_x_two(up, down):
    return move_x(up, 1), move_x(down, -1)


def near_y_two(up, down):
    return move_y(up, 1), move_y(down, -1)


def reduce_y_first(values, z, y):
    far = (y + 2) & 3
    return move_y(pick(values, z, far), 1), move_y(pick(values, 1 - z, far), -1)


def reduce_y_ready(values, z, y, first):
    up, down = first
    other, y_after, y_before = 1 - z, (y + 1) & 3, (y - 1) & 3
    after_it = jnp.stack([added(pick(values, z, y_after), up), pick(values, other, y_after)])
    before = jnp.stack([pick(values, z, y_before), added(pick(values, other, y_before), down)])
    return after_it, before


def reduce_y_second(values, z, y, first):
    return near_y_two(*reduce_y_ready(values, z, y, first))


def reduce_z(values, z, y, second):
    def total(k, zi):
        own = pick(values, zi, y)
        return (own.astype(f32) + second[0][k].astype(f32) + second[1][k].astype(f32)).astype(low)

    return added(total(0, z), swap_z(total(1, 1 - z)))


def by_chip(gradient):
    return gradient.reshape(2, 4, gradient.shape[0] // 8, gradient.shape[1])


def quarters(value):
    return value.reshape(4, value.shape[0] // 4, value.shape[1])


def gather_x(value, x):
    cut = value.shape[0] // 2
    behind, ahead = move_x(value, 1), move_x(value, -1)
    far = jnp.concatenate([move_x(behind[:cut], 1), move_x(ahead[cut:], -1)])
    ring = jnp.stack([value, ahead, far, behind, value, ahead, far, behind])
    return lax.dynamic_slice_in_dim(ring, (4 - x) & 3, 4, 0)


def packed(value):
    return jnp.concatenate([value[:, k : k + 512] for k in range(0, value.shape[1], 512)])


def unpacked(rows, part, width):
    blocks = [rows[:, k * part : (k + 1) * part] for k in range(width // 512)]
    return jnp.concatenate(blocks, axis=2).reshape(4 * part, width)


def finish(values, x, core):
    sizes = [v.shape for v in values]
    together = gather_x(jnp.concatenate([packed(v) for v in values]), x)
    chips, at = [], 0
    for part, width in sizes:
        n = part * width // 512
        chip = unpacked(together[:, at : at + n], part, width)
        if width == 3072:
            blocks = chip.reshape(4, part, 4, width // 4).transpose(2, 1, 0, 3)
            chip = blocks.reshape(4 * part, width)
        chips.append(chip)
        at += n
    mine = [half_of(chip, core, 0) for chip in chips]
    theirs = [half_of(chip, 1 - core, 0) for chip in chips]
    arrived = swap_core(jnp.concatenate([packed(t) for t in theirs]))
    outs, at = [], 0
    for (part, width), own in zip(sizes, mine):
        n = 2 * part * width // 512
        rows = arrived[at : at + n]
        at += n
        other = jnp.concatenate(
            [rows[k * 2 * part : (k + 1) * 2 * part] for k in range(width // 512)], axis=1
        )
        outs.append((own.astype(f32), other.astype(f32)))
    return outs


def row_scale(values):
    return lax.rsqrt(jnp.mean(values * values, axis=-1, keepdims=True) + epsilon)


def rotation_tables(length):
    half_size = HEAD // 2
    places = jnp.arange(length, dtype=f32)
    frequencies = rope_base ** (-jnp.arange(half_size, dtype=f32) * 2.0 / HEAD)
    angles = places[:, None] * frequencies[None, :]
    cosine, sine = jnp.cos(angles), jnp.sin(angles)
    return jnp.concatenate([cosine, cosine], 1), jnp.concatenate([-sine, sine], 1)


def norm_backward(upstream, normed, scaling, gain_vector):
    gain_part = jnp.sum(upstream * normed, axis=tuple(range(upstream.ndim - 1)))
    scaled = upstream * gain_vector
    return (
        scaling * (scaled - normed * jnp.mean(scaled * normed, axis=-1, keepdims=True)),
        gain_part,
    )


def dot(left, right):
    return jnp.dot(left, right, preferred_element_type=f32)


def dot_t(left, right):
    return lax.dot_general(left, right, (((1,), (1,)), ((), ())), preferred_element_type=f32)


def dot_first(left, right):
    return lax.dot_general(left, right, (((0,), (0,)), ((), ())), preferred_element_type=f32)


def turned(values, cosine, sine):
    return values * cosine + pltpu.roll(values, HEAD // 2, 1) * sine


def scaled_heads(qkv, query_gain, key_gain, cosine, sine):
    q = jnp.concatenate([qkv[:, :HEAD], qkv[:, HEAD : 2 * HEAD]])
    k, v = qkv[:, 2 * HEAD : 3 * HEAD], qkv[:, 3 * HEAD :].astype(low)
    q_scale, k_scale = row_scale(q), row_scale(k)
    qn, kn = q * q_scale, k * k_scale
    cosine_two, sine_two = jnp.concatenate([cosine] * 2), jnp.concatenate([sine] * 2)
    qr = turned(qn * query_gain, cosine_two, sine_two).astype(low)
    kr = turned(kn * key_gain, cosine, sine).astype(low)
    return qr, kr, v, qn, kn, q_scale, k_scale


def soft_scores(qr, kr):
    scores = dot_t(qr, kr) * ROOT
    query = lax.broadcasted_iota(jnp.int32, scores.shape, 0) & 127
    key = lax.broadcasted_iota(jnp.int32, scores.shape, 1)
    scores = jnp.where(query >= key, scores, -1e30)
    p = jnp.exp(scores - jnp.max(scores, axis=-1, keepdims=True))
    return p / jnp.sum(p, axis=-1, keepdims=True)


def attention_kernel(first, *refs):
    if first:
        hidden, gain, qg, kg, cosine, sine, w, wo, out, a1, qkv_out, att_out = refs
    else:
        sofar, a1, qg, kg, cosine, sine, w, wo, out, qkv_out, att_out = refs

    @pl.when(pl.program_id(0) == 0)
    def _():
        if first:
            h = hidden[...]
            a1[...] = (h * row_scale(h) * gain[...]).astype(low)
            out[...] = h
        else:
            out[...] = sofar[...]

    qkv = dot(a1[...], w[...])
    qkv_out[...] = qkv
    for s in range(2):
        rows = slice(128 * s, 128 * s + 128)
        qr, kr, v, *_ = scaled_heads(qkv[rows], qg[...], kg[...], cosine[...], sine[...])
        att = dot(soft_scores(qr, kr).astype(low), v).astype(low)
        att_out[rows, :HEAD] = att[:128]
        att_out[rows, HEAD:] = att[128:]
    out[...] += dot(att_out[...], wo[...])


def whole(shape):
    return pl.BlockSpec(shape, lambda i: (0,) * len(shape))


def columns_at(rows, width):
    return pl.BlockSpec((rows, width), lambda i: (0, i))


def rows_at(rows, width, start):
    return pl.BlockSpec((rows, width), lambda i: (start + i, 0))


def shape_of(rows, width, kind):
    return jax.ShapeDtypeStruct((rows, width), kind)


def call(kernel, steps, ins, outs, waits=()):
    specs, values = [p[0] for p in ins], [p[1] for p in ins]
    specs += [pl.BlockSpec(memory_space=pl.ANY)] * len(waits)
    values += list(waits)

    def body(*refs):
        kernel(*refs[: len(ins)], *refs[len(ins) + len(waits) :])

    return pl.pallas_call(
        body,
        grid=(steps,),
        in_specs=specs,
        out_specs=[p[0] for p in outs],
        out_shape=[p[1] for p in outs],
        compiler_params=pltpu.CompilerParams(vmem_limit_bytes=28 * 2**20),
        cost_estimate=pl.CostEstimate(flops=2**20, bytes_accessed=2**16, transcendentals=0),
    )(*values)


BLOCK = (256, MODEL)


def attention_half(half, state, w_half, w_out, gains, tables, waits=()):
    mixer_gain, query_gain, key_gain, _ = gains
    head, table = whole((1, HEAD)), whole((128, HEAD))
    ins = [(whole(BLOCK), state[0])]
    ins.append((whole((1, MODEL)), mixer_gain[None]) if half == 0 else (whole(BLOCK), state[1]))
    ins += [(head, query_gain[None]), (head, key_gain[None]), (table, tables[0]), (table, tables[1])]
    ins += [(columns_at(MODEL, 512), w_half), (rows_at(256, MODEL, 4 * half), w_out)]
    outs = [(whole(BLOCK), shape_of(*BLOCK, f32))]
    if half == 0:
        outs.append((whole(BLOCK), shape_of(*BLOCK, low)))
    outs.append((columns_at(256, 512), shape_of(256, 2048, f32)))
    outs.append((columns_at(256, 256), shape_of(256, 1024, low)))
    return call(functools.partial(attention_kernel, half == 0), 4, ins, outs, waits)


def dense_kernel(first, *refs):
    if first:
        hidden, gain, w, wd, out, a2, gu_out, z_out = refs
    else:
        sofar, a2, w, wd, out, gu_out, z_out = refs

    @pl.when(pl.program_id(0) == 0)
    def _():
        if first:
            h = hidden[...]
            a2[...] = (h * row_scale(h) * gain[...]).astype(low)
            out[...] = h
        else:
            out[...] = sofar[...]

    gu = dot(a2[...], w[...])
    gu_out[...] = gu.astype(gu_out.dtype)
    gate, up = gu[:, :512], gu[:, 512:]
    z = (gate * jax.nn.sigmoid(gate) * up).astype(low)
    z_out[...] = z
    out[...] += dot(z, wd[...])


def dense_half(half, state, w_half, w_down, gains):
    ins = [(whole(BLOCK), state[0])]
    ins.append((whole((1, MODEL)), gains[3][None]) if half == 0 else (whole(BLOCK), state[1]))
    ins += [(columns_at(MODEL, 1024), w_half), (rows_at(512, MODEL, 3 * half), w_down)]
    outs = [(whole(BLOCK), shape_of(*BLOCK, f32))]
    if half == 0:
        outs.append((whole(BLOCK), shape_of(*BLOCK, low)))
    outs.append((columns_at(256, 1024), shape_of(256, 3072, f32)))
    outs.append((columns_at(256, 512), shape_of(256, 1536, low)))
    return call(functools.partial(dense_kernel, half == 0), 3, ins, outs)


def forward_mixer(hidden, w_qkv, w_out, gains, tables, between=None):
    part, a1, qkv_0, att_0 = attention_half(0, (hidden,), w_qkv[0], w_out, gains, tables)
    waits = between(part) if between is not None else ()
    after_mixer, qkv_1, att_1 = attention_half(1, (part, a1), w_qkv[1], w_out, gains, tables, waits)
    return after_mixer, (hidden, a1, (qkv_0, qkv_1), (att_0, att_1), after_mixer)


def forward_dense(after_mixer, w_gu, w_down, gains):
    part, a2, gu_0, z_0 = dense_half(0, (after_mixer,), w_gu[0], w_down, gains)
    out, gu_1, z_1 = dense_half(1, (part, a2), w_gu[1], w_down, gains)
    return out, (a2, (gu_0, gu_1), (z_0, z_1))


def forward(hidden, weights, gains, tables):
    w_qkv, w_out, w_gu, w_down = weights
    after_mixer, saved = forward_mixer(hidden, w_qkv, w_out, gains, tables)
    out, saved_dense = forward_dense(after_mixer, w_gu, w_down, gains)
    return out, saved + saved_dense


def dense_back_kernel(first, *refs):
    sofar, refs = (None, refs) if first else (refs[0], refs[1:])
    dm, wd, gu, w, dgu_out, da2 = refs

    @pl.when(pl.program_id(0) == 0)
    def _():
        da2[...] = jnp.zeros_like(da2) if first else sofar[...]

    dz = dot_t(dm[...], wd[...])
    gate, up = gu[:, :512], gu[:, 512:]
    sig = jax.nn.sigmoid(gate)
    dg = (dz * up * sig * (1.0 + gate * (1.0 - sig))).astype(low)
    du = (dz * (gate * sig)).astype(low)
    dgu_out[:, :512] = dg
    dgu_out[:, 512:] = du
    da2[...] += dot_t(dgu_out[...], w[...])


def dense_back_half(half, sofar, dm, gu, w_half, w_down):
    ins = [] if half == 1 else [(whole(BLOCK), sofar)]
    ins += [(whole(BLOCK), dm), (rows_at(512, MODEL, 3 * half), w_down)]
    ins += [(columns_at(256, 1024), gu), (columns_at(MODEL, 1024), w_half)]
    outs = [(columns_at(256, 1024), shape_of(256, 3072, low)), (whole(BLOCK), shape_of(*BLOCK, f32))]
    kernel = functools.partial(dense_back_kernel, half == 1)
    return call(kernel, 3, ins, outs)


def normed_back(upstream, normed, scale, gain):
    gain_part = jnp.sum(upstream * normed, axis=0, keepdims=True)
    scaled = upstream * gain
    return scale * (scaled - normed * jnp.mean(scaled * normed, axis=-1, keepdims=True)), gain_part


def attention_back_kernel(first, *refs):
    sofar, refs = (None, refs) if first else (refs[:3], refs[3:])
    dr, wo, qkv, qg, kg, cosine, sine, w, dqkv_out, da1, q_grad, k_grad = refs

    @pl.when(pl.program_id(0) == 0)
    def _():
        for k, ref in enumerate((da1, q_grad, k_grad)):
            ref[...] = jnp.zeros_like(ref) if first else sofar[k][...]

    datt = dot_t(dr[...], wo[...]).astype(low)
    for s in range(2):
        rows = slice(128 * s, 128 * s + 128)
        cos, sin = cosine[...], sine[...]
        qr, kr, v, qn, kn, q_scale, k_scale = scaled_heads(qkv[rows, :], qg[...], kg[...], cos, sin)
        p = soft_scores(qr, kr)
        do = jnp.concatenate([datt[rows, :HEAD], datt[rows, HEAD:]])
        dp = dot_t(do, v)
        dv = dot_first(p.astype(low), do)
        ds = (p * (dp - jnp.sum(dp * p, axis=-1, keepdims=True))).astype(low)
        dqr, dkr = dot(ds, kr) * ROOT, dot_first(ds, qr) * ROOT
        cos_two, sin_two = jnp.concatenate([cos] * 2), jnp.concatenate([sin] * 2)
        dq, q_part = normed_back(turned(dqr, cos_two, -sin_two), qn, q_scale, qg[...])
        dk, k_part = normed_back(turned(dkr, cos, -sin), kn, k_scale, kg[...])
        q_grad[...] += q_part
        k_grad[...] += k_part
        dq = dq.astype(low)
        dqkv_out[rows, :HEAD] = dq[:128]
        dqkv_out[rows, HEAD : 2 * HEAD] = dq[128:]
        dqkv_out[rows, 2 * HEAD : 3 * HEAD] = dk.astype(low)
        dqkv_out[rows, 3 * HEAD :] = dv.astype(low)
    da1[...] += dot_t(dqkv_out[...], w[...])


def attention_back_half(half, sofar, dr, qkv, w_half, w_out, gains, tables, waits=()):
    head, table = whole((1, HEAD)), whole((128, HEAD))
    ins = [] if half == 1 else [(whole(BLOCK), sofar[0]), (head, sofar[1]), (head, sofar[2])]
    ins += [(whole(BLOCK), dr), (rows_at(256, MODEL, 4 * half), w_out), (columns_at(256, 512), qkv)]
    ins += [(head, gains[1][None]), (head, gains[2][None]), (table, tables[0]), (table, tables[1])]
    ins += [(columns_at(MODEL, 512), w_half)]
    outs = [(columns_at(256, 512), shape_of(256, 2048, low)), (whole(BLOCK), shape_of(*BLOCK, f32))]
    outs += [(head, shape_of(1, HEAD, f32))] * 2
    kernel = functools.partial(attention_back_kernel, half == 1)
    return call(kernel, 4, ins, outs, waits)


def backward(cotangent, saved, weights, gains, tables, between=None):
    w_qkv, w_out, w_gu, w_down = weights
    mixer_gain, query_gain, key_gain, dense_gain = gains
    hidden, a1, qkv, att, after_mixer, a2, gu, z = saved
    dm = cotangent.astype(low)
    dgu_1, da2 = dense_back_half(1, None, dm, gu[1], w_gu[1], w_down)
    dgu_0, da2 = dense_back_half(0, da2, dm, gu[0], w_gu[0], w_down)
    if between is not None:
        da2 = between[0]((dgu_0, dgu_1), da2)
    scale_two = row_scale(after_mixer)
    part, dense_gain_grad = norm_backward(da2, after_mixer * scale_two, scale_two, dense_gain)
    dh2 = cotangent + part
    dr = dh2.astype(low)
    g_out = None
    if between is not None:
        dr, g_out = between[1](dr)
    dqkv_1, *so_far = attention_back_half(1, None, dr, qkv[1], w_qkv[1], w_out, gains, tables)
    if between is not None:
        dr = between[3](dr, dqkv_1, g_out)
    dqkv_0, da1, q_grad, k_grad = attention_back_half(
        0, so_far, dr, qkv[0], w_qkv[0], w_out, gains, tables
    )
    if between is not None:
        da1 = between[2]((dqkv_0, dqkv_1), da1, g_out)
    scale_one = row_scale(hidden)
    part, mixer_gain_grad = norm_backward(da1, hidden * scale_one, scale_one, mixer_gain)
    dh = dh2 + part
    return dh, (mixer_gain_grad, dense_gain_grad, q_grad[0], k_grad[0])


def product(left, left_other, right, right_other):
    both_left = jnp.concatenate([left, left_other])
    both_right = jnp.concatenate([right, right_other])
    dims = (((0,), (0,)), ((), ()))
    return lax.dot_general(both_left, both_right, dims, preferred_element_type=f32).astype(low)


def on_device(
    boundary,
    mixer_gain,
    query_weight,
    key_weight,
    value_weight,
    output_weight,
    query_gain,
    key_gain,
    dense_gain,
    gate_weight,
    up_weight,
    down_weight,
):
    first_section = lax.axis_index("section") == 0
    x = lax.axis_index("dp")
    place_at = lax.axis_index("fsdp")
    core, y, z = place_at & 1, (place_at >> 1) & 3, place_at >> 3
    spot = (x, z, y)
    local = boundary[0, :, 0].astype(f32).reshape(256, MODEL)

    gain_tile = jnp.stack(
        [mixer_gain[0], dense_gain[0], jnp.pad(query_gain[0], (0, 56)), jnp.pad(key_gain[0], (0, 56))],
        axis=1,
    )
    gain_tile = jnp.pad(gain_tile, ((0, 0), (0, 124)))

    def column_half(index):
        def cut(value):
            return half_of(value[0], index, 1)

        def mixed(parts, widths):
            halves = [cut(p) for p in parts]
            blocks = range(halves[0].shape[1] // widths[0])
            return [h[:, b * w : (b + 1) * w] for b in blocks for h, w in zip(halves, widths)]

        def rows_beside(value):
            half = cut(value)
            return [half[k : k + 64] for k in range(0, half.shape[0], 64)]

        pieces = mixed((query_weight, key_weight, value_weight), (256, 128, 128)) + [gain_tile]
        pieces += rows_beside(output_weight)
        pieces += mixed((gate_weight, up_weight), (512, 512)) + rows_beside(down_weight)
        return jnp.concatenate(pieces, axis=1)

    chip = in_order(column_half(core), swap_core(column_half(1 - core)), core, 0)
    zero = jnp.zeros_like(z)
    z_own = z ^ core

    with jax.named_scope("ag_dense"):
        d_0 = lax.dynamic_slice(chip, (x * 32, zero + 3200), (32, 4608))
        d_z = swap_z(d_0)
        d_pair = jnp.stack([d_0, d_z])
        d_near = near_y(d_pair)
        m_0 = chip[:, :3200]
        m_z = swap_z(m_0)
        d_near, m_z = tied(d_near, m_z)
        d_far = far_y(*d_near)
        d_all = jnp.concatenate([d_pair, *d_near, *d_far])
        d_x = near_x(d_all)
    with jax.named_scope("ag_mixer"):
        m_pair = jnp.stack([m_0, m_z])
        m_near = near_y(m_pair)
        m_near, d_x = tied(m_near, d_x)
        m_far = far_y(*m_near)
        moves, offsets = [], []
        spots = [(0, 0), (0, 1), (1, 0), (1, 1), (2, 0), (2, 1), (3, 0), (4, 0)]
        for (piece, index), (dz, dy) in zip(spots, origins):
            moves.append((piece, index, 0, 0, 128, 2176, 0))
            offsets.append(((z ^ dz) * 4 + ((y - dy) & 3)) * 128)
            block = ((z_own ^ dz) * 4 + ((y - dy) & 3)) * 256
            for k in range(2):
                for m in range(2):
                    moves.append((piece, index, 64 * k, 2176 + 512 * m, 64, 512, 1))
                    offsets.append(block + 128 * k + 64 * m)
        own_qkv, own_out = place(
            (m_pair, *m_near, *m_far), moves, offsets, ((MODEL, 2176), (2048, 512))
        )
        w_qkv = (own_qkv, swap_core(own_qkv))
        w_out = joined(own_out, core)
    tile = own_qkv[:, 2048:2052].astype(f32)
    gains = (
        tile[:, 0],
        tile[:, 2].reshape(16, 64)[:, :8].reshape(HEAD),
        tile[:, 3].reshape(16, 64)[:, :8].reshape(HEAD),
        tile[:, 1],
    )
    tables = rotation_tables(128)
    d_x_far = far_x(*d_x)

    def place_dense(part):
        moves, offsets = [], []
        for piece, dx in enumerate((0, 1, 3, 2, 2)):
            turn = (x - dx) & 3
            kept = range(4) if piece == 3 else range(4, 8) if piece == 4 else range(8)
            for index, n in enumerate(kept):
                dz, dy = origins[n]
                moves.append((piece, index, 0, 0, 32, 3072, 0))
                offsets.append(((z ^ dz) * 4 + ((y - dy) & 3)) * 128 + turn * 32)
                block = ((z_own ^ dz) * 4 + ((y - dy) & 3)) * 384 + (turn >> 1) * 192
                for m in range(3):
                    moves.append((piece, index, 0, 3072 + 512 * m, 32, 512, 1))
                    offsets.append(block + 64 * m + (turn & 1) * 32)
        return place((d_all, *d_x, *d_x_far), moves, offsets, ((MODEL, 3072), (3072, 512)), (part,))

    own_dense = []

    def between_halves(part):
        own_dense.extend(place_dense(part))
        return (own_dense[0],)

    with jax.named_scope("f1"):
        early_mixer, _ = forward_mixer(local, w_qkv, w_out, gains, tables, between_halves)
    with jax.named_scope("ag_dense"):
        own_gu, own_down = own_dense
        w_gu = (own_gu, swap_core(own_gu))
        w_down = joined(own_down, core)
    weights = (w_qkv, w_out, w_gu, w_down)
    with jax.named_scope("f1"):
        early, _ = forward_dense(early_mixer, w_gu, w_down, gains)
    arrived = move_section(early.astype(low), 1).astype(f32)
    with jax.named_scope("f2"):
        out, saved = forward(jnp.where(first_section, local, arrived), weights, gains, tables)
    _, a1, _, att, _, a2, _, z_low = saved
    with jax.named_scope("b1"):
        early_dh, _ = backward(local, saved, weights, gains, tables)
    returned = move_section(early_dh.astype(low), -1).astype(f32)
    cotangent = jnp.where(first_section, returned, local)

    acts = jnp.concatenate([a1, att[1], att[0], a2, z_low[1], z_low[0]], axis=1)
    acts = swap_core(acts)
    a1_o, att_o = acts[:, :1024], (acts[:, 1024:2048], acts[:, 2048:3072])
    a2_o, z_o = acts[:, 3072:4096], (acts[:, 4096:5632], acts[:, 5632:])

    def by_halves(left, left_other, right, right_other):
        parts = [product(a, b, right, right_other) for a, b in zip(left, left_other)]
        return by_chip(jnp.concatenate(parts))

    cot_mine, cot_theirs = half_of(cotangent, core, 1), half_of(cotangent, 1 - core, 1)
    z_flip = z ^ core
    done = {}

    def after_dgu(dgu, da2):
        with jax.named_scope("g_gu"):
            g_gu = product(a2, a2_o, dgu[0], swap_core(dgu[1])).reshape(8, 128, 3072)
            da2, g_gu = tied(da2, g_gu)

            def columns_of(place):
                return lax.dynamic_slice_in_dim(g_gu, place * 768, 768, 2)

            done["gu"] = (columns_of, reduce_x_first(columns_of, x))
        with jax.named_scope("g_down"):
            dm_o = swap_core(cot_theirs.astype(low))
            g_down = by_halves(z_low, z_o, cot_mine.astype(low), dm_o)
            da2, g_down = tied(da2, g_down)
            done["down"] = g_down
        return da2

    def after_dr(dr):
        with jax.named_scope("g_out"):
            dr_o = swap_core(half_of(dr, 1 - core, 1))
            g_out = by_halves(att, att_o, half_of(dr, core, 1), dr_o)
            g_do = jnp.concatenate([done["down"], g_out], axis=2)
        with jax.named_scope("rs_do"):
            done["do"] = reduce_y_first(g_do, z_flip, y)
        with jax.named_scope("rs_gu"):
            columns_of, first = done["gu"]
            ready = reduce_x_ready(columns_of, x, first)
            dr, ready, g_do = tied(dr, ready, g_do)
            done["gu2"] = near_x_two(*ready)
        return dr, g_do

    def between_heads(dr, dqkv_1, g_do):
        with jax.named_scope("g_qkv"):
            done["dqkv_o"] = swap_core(dqkv_1)
        with jax.named_scope("rs_do"):
            first, dqkv_1 = tied(done["do"], dqkv_1)
            ready = reduce_y_ready(g_do, z_flip, y, first)
            dr, ready = tied(dr, ready)
            done["do2"] = near_y_two(*ready)
        return dr

    def after_attention(dqkv, da1, g_do):
        own, second_gu, second = tied(dqkv[0], done["gu2"], done["do2"])
        with jax.named_scope("g_qkv"):
            g_qkv = by_chip(product(a1, a1_o, own, done["dqkv_o"]))
        with jax.named_scope("rs_qg"):
            mine = reduce_x_third(done["gu"][0], x, second_gu).reshape(2, 4, 128, 768)
            both_parts = jnp.concatenate([g_qkv, mine], axis=3)
            da1, both_parts = tied(da1, both_parts)
            done["qg"] = (both_parts, reduce_y_first(both_parts, z, y))
        with jax.named_scope("rs_do"):
            done["s_do"] = reduce_z(g_do, z_flip, y, second)
        return da1

    with jax.named_scope("b2"):
        dh, gain_grads = backward(
            cotangent, saved, weights, gains, tables, (after_dgu, after_dr, after_attention, between_heads)
        )
    endpoints = jnp.where(first_section, dh, out).reshape(1, 2, 1, 128, MODEL)
    with jax.named_scope("rs_qg"):
        g_qg, first = done["qg"]
        s_qg = reduce_z(g_qg, z, y, reduce_y_second(g_qg, z, y, first))
    with jax.named_scope("rs_x"):
        s_do, s_qkv = quarters(done["s_do"][:384]), quarters(s_qg[:, :2048])
        s_o = quarters(done["s_do"][384:])
        blocks = [s_qkv[:, :, k : k + 512] for k in range(0, 2048, 512)] + [s_do, s_o]
        mine = reduce_x(jnp.concatenate(blocks, axis=1), x)
        m_qkv = jnp.concatenate([mine[k : k + 32] for k in range(0, 128, 32)], axis=1)
        m_gu = jnp.concatenate([s_qg[k : k + 32, 2048:] for k in range(0, 128, 32)], axis=1)
    with jax.named_scope("fin"):
        parts = (m_qkv, m_gu, mine[128:224], mine[224:])
        qkv, gu, down, out_w = finish(parts, x, core)

    def both(pair, start, width, block=None):
        block = block or pair[0].shape[1]

        def part(value):
            starts = range(start, value.shape[1], block)
            return jnp.concatenate([value[:, k : k + width] for k in starts], axis=1)

        return in_order(*(part(p) for p in pair), core, 1)[None]

    sums = summed(jnp.concatenate(gain_grads).reshape(18, 128)).reshape(-1)

    def gain_rows(start, width):
        return lax.dynamic_slice_in_dim(sums, start + place_at * width, width, 0)[None]

    return (
        endpoints,
        gain_rows(0, 64),
        both(qkv, 0, 256, 512),
        both(qkv, 256, 128, 512),
        both(qkv, 384, 128, 512),
        both(out_w, 0, 512),
        gain_rows(2048, 8),
        gain_rows(2176, 8),
        gain_rows(1024, 64),
        both(gu, 0, 512, 1024),
        both(gu, 512, 512, 1024),
        both(down, 0, 512),
    )


def solution(mesh):
    placed = (
        P("section", None, ("dp", "fsdp"), None, None),
        P("section", "fsdp"),
        P("section", "fsdp", None),
        P("section", "fsdp", None),
        P("section", "fsdp", None),
        P("section", "fsdp", None),
        P("section", "fsdp"),
        P("section", "fsdp"),
        P("section", "fsdp"),
        P("section", "fsdp", None),
        P("section", "fsdp", None),
        P("section", "fsdp", None),
    )
    return jax.shard_map(
        on_device,
        mesh=mesh,
        in_specs=placed,
        out_specs=(
            P("section", None, ("dp", "fsdp"), None, None),
            P("section", "fsdp"),
            P("section", "fsdp", None),
            P("section", "fsdp", None),
            P("section", "fsdp", None),
            P("section", "fsdp", None),
            P("section", "fsdp"),
            P("section", "fsdp"),
            P("section", "fsdp"),
            P("section", "fsdp", None),
            P("section", "fsdp", None),
            P("section", "fsdp", None),
        ),
        check_vma=False,
    )
```

```python
import functools

import jax
import jax.numpy as jnp
from jax import lax
from jax.experimental import pallas as pl
from jax.experimental.pallas import tpu as pltpu
from jax.sharding import PartitionSpec as P

epsilon = 1e-06
rope_base = 1000000.0
low = jnp.bfloat16
f32 = jnp.float32
MODEL = 1024
HEAD = 128
ROOT = HEAD ** (-0.5)


def tied(*values):
    return lax.optimization_barrier(values)


def swap_core(value):
    return lax.ppermute(value, "fsdp", [(i, i ^ 1) for i in range(16)])


def swap_z(value):
    return lax.ppermute(value, "fsdp", [(i, i ^ 8) for i in range(16)])


def move_y(value, step):
    pairs = [(i, (i & 8) | ((((i >> 1) + step) & 3) << 1) | (i & 1)) for i in range(16)]
    return lax.ppermute(value, "fsdp", pairs)


def move_x(value, step):
    return lax.ppermute(value, "dp", [(i, (i + step) % 4) for i in range(4)])


def move_section(value, step):
    return lax.ppermute(value, "section", [(0, 1)] if step > 0 else [(1, 0)])


def summed_x(value):
    for step in (1, 2):
        value = value + lax.ppermute(value, "dp", [(i, i ^ step) for i in range(4)])
    return value


def summed_over(value, *steps):
    for step in steps:
        value = value + lax.ppermute(value, "fsdp", [(i, i ^ step) for i in range(16)])
    return value


def pick(value, *where):
    start = list(where) + [0] * (value.ndim - len(where))
    size = [1] * len(where) + list(value.shape[len(where) :])
    return lax.dynamic_slice(value, start, size).reshape(value.shape[len(where) :])


def half_of(value, index, axis):
    width = value.shape[axis] // 2
    return lax.dynamic_slice_in_dim(value, index * width, width, axis)


def in_order(own, other, core, axis):
    first = jnp.where(core == 0, own, other)
    second = jnp.where(core == 0, other, own)
    return jnp.concatenate([first, second], axis=axis)


def placing_kernel(moves, sources_count, skipped, offsets, *refs):
    sources, outs, sems = refs[:sources_count], refs[sources_count + skipped : -1], refs[-1]
    copies = []
    for n, (source, index, row, column, rows, width, out) in enumerate(moves):
        block = sources[source].at[index, pl.ds(row, rows), pl.ds(column, width)]
        at = pl.multiple_of(offsets[n], 16)
        copies.append(pltpu.make_async_copy(block, outs[out].at[pl.ds(at, rows)], sems.at[n]))
    for copy in copies:
        copy.start()
    for copy in copies:
        copy.wait()


def place(pieces, moves, offsets, shapes, waits=()):
    return pl.pallas_call(
        functools.partial(placing_kernel, tuple(moves), len(pieces), len(waits)),
        out_shape=[jax.ShapeDtypeStruct(shape, low) for shape in shapes],
        in_specs=[pl.BlockSpec(memory_space=pltpu.SMEM)]
        + [pl.BlockSpec(memory_space=pl.ANY)] * (len(pieces) + len(waits)),
        out_specs=[pl.BlockSpec(memory_space=pltpu.VMEM)] * len(shapes),
        scratch_shapes=[pltpu.SemaphoreType.DMA((len(moves),))],
        compiler_params=pltpu.CompilerParams(vmem_limit_bytes=16 * 2**20),
        cost_estimate=pl.CostEstimate(flops=2**20, bytes_accessed=2**16, transcendentals=0),
    )(jnp.stack(offsets).astype(jnp.int32), *pieces, *waits)


def packing_kernel(moves, count, core_ref, *refs):
    sources, outs, sems = refs[:count], refs[count:-1], refs[-1]
    copies = []
    for k, out in enumerate(outs):
        half = core_ref[0] if k == 0 else 1 - core_ref[0]
        for n, (source, row, half_width, column, width, at) in enumerate(moves):
            start = pl.multiple_of(half * half_width + column, 128)
            block = sources[source].at[pl.ds(row, 64), pl.ds(start, width)]
            sem = sems.at[k * len(moves) + n]
            copies.append(pltpu.make_async_copy(block, out.at[:, pl.ds(at, width)], sem))
    for copy in copies:
        copy.start()
    for copy in copies:
        copy.wait()


def pack_halves(weights, gain_tile, core):
    q, k, v, out, gate, up, down = weights
    moves = []
    for b in range(4):
        moves += [(0, 0, 1024, 256 * b, 256), (1, 0, 512, 128 * b, 128), (2, 0, 512, 128 * b, 128)]
    moves.append((7, 0, 0, 0, 128))
    moves += [(3, 64 * m, 512, 0, 512) for m in range(2)]
    for b in range(3):
        moves += [(4, 0, 1536, 512 * b, 512), (5, 0, 1536, 512 * b, 512)]
    moves += [(6, 64 * m, 512, 0, 512) for m in range(3)]
    at, placed = 0, []
    for move in moves:
        placed.append((*move, at))
        at += move[-1]
    shape = jax.ShapeDtypeStruct((64, at), low)
    return pl.pallas_call(
        functools.partial(packing_kernel, tuple(placed), 8),
        out_shape=[shape, shape],
        in_specs=[pl.BlockSpec(memory_space=pltpu.SMEM)] + [pl.BlockSpec(memory_space=pl.ANY)] * 8,
        out_specs=[pl.BlockSpec(memory_space=pltpu.VMEM)] * 2,
        scratch_shapes=[pltpu.SemaphoreType.DMA((2 * len(placed),))],
        compiler_params=pltpu.CompilerParams(vmem_limit_bytes=8 * 2**20),
    )(core.reshape(1).astype(jnp.int32), q, k, v, out, gate, up, down, gain_tile)


def joining_kernel(core_ref, own, other, out, sems):
    rows, width = own.shape
    cut = rows // 2
    mine = pl.multiple_of(core_ref[0] * width, width)
    theirs = pl.multiple_of((1 - core_ref[0]) * width, width)
    upper, lower = pl.ds(0, cut), pl.ds(cut, cut)
    copies = (
        pltpu.make_async_copy(own, out.at[:, pl.ds(mine, width)], sems.at[0]),
        pltpu.make_async_copy(other.at[lower], out.at[upper, pl.ds(theirs, width)], sems.at[1]),
        pltpu.make_async_copy(other.at[upper], out.at[lower, pl.ds(theirs, width)], sems.at[2]),
    )
    for copy in copies:
        copy.start()
    for copy in copies:
        copy.wait()


def joined(own, core):
    rows, width = own.shape
    return pl.pallas_call(
        joining_kernel,
        out_shape=jax.ShapeDtypeStruct((rows, 2 * width), low),
        in_specs=[pl.BlockSpec(memory_space=pltpu.SMEM)] + [pl.BlockSpec(memory_space=pl.ANY)] * 2,
        out_specs=pl.BlockSpec(memory_space=pltpu.VMEM),
        scratch_shapes=[pltpu.SemaphoreType.DMA((3,))],
        compiler_params=pltpu.CompilerParams(vmem_limit_bytes=16 * 2**20),
        cost_estimate=pl.CostEstimate(flops=2**20, bytes_accessed=2**16, transcendentals=0),
    )(core.reshape(1).astype(jnp.int32), own, swap_core(own))


origins = [(0, 0), (1, 0), (0, 1), (1, 1), (0, 3), (1, 3), (0, 2), (1, 2)]


def near_y(pair):
    return move_y(pair, 1), move_y(pair, -1)


def far_y(behind, ahead):
    return move_y(behind[0], 1)[None], move_y(ahead[1], -1)[None]


def near_x(first, second):
    return move_x(first, 1), move_x(second, 1), move_x(first, -1), move_x(second, -1)


def far_x(behind_first, behind_second, ahead_first, ahead_second):
    return move_x(behind_first, 1), move_x(ahead_second, -1)


def added(left, right):
    return (left.astype(f32) + right.astype(f32)).astype(low)


def reduce_x_first(take, x):
    far = take((x + 2) & 3)
    cut = far.shape[0] // 2
    return move_x(far[:cut], 1), move_x(far[cut:], -1)


def reduce_x_ready(take, x, first):
    up, down = first
    cut = up.shape[0]
    after_it, before = take((x + 1) & 3), take((x - 1) & 3)
    after_it = jnp.concatenate([added(after_it[:cut], up), after_it[cut:]])
    before = jnp.concatenate([before[:cut], added(before[cut:], down)])
    return after_it, before


def reduce_x_third(take, x, second):
    own = take(x)
    return (own.astype(f32) + second[0].astype(f32) + second[1].astype(f32)).astype(low)


def reduce_x(values, x):
    def take(place):
        return pick(values, place)

    second = near_x_two(*reduce_x_ready(take, x, reduce_x_first(take, x)))
    return reduce_x_third(take, x, second)


def near_x_two(up, down):
    return move_x(up, 1), move_x(down, -1)


def near_y_two(up, down):
    return move_y(up, 1), move_y(down, -1)


def reduce_y_first(values, z, y):
    far = (y + 2) & 3
    return move_y(pick(values, z, far), 1), move_y(pick(values, 1 - z, far), -1)


def reduce_y_ready(values, z, y, first):
    up, down = first
    other, y_after, y_before = 1 - z, (y + 1) & 3, (y - 1) & 3
    after_it = jnp.stack([added(pick(values, z, y_after), up), pick(values, other, y_after)])
    before = jnp.stack([pick(values, z, y_before), added(pick(values, other, y_before), down)])
    return after_it, before


def reduce_y_second(values, z, y, first):
    return near_y_two(*reduce_y_ready(values, z, y, first))


def reduce_z(values, z, y, second):
    def total(k, zi):
        own = pick(values, zi, y)
        return (own.astype(f32) + second[0][k].astype(f32) + second[1][k].astype(f32)).astype(low)

    return total(0, z), swap_z(total(1, 1 - z))


def by_chip(gradient):
    return gradient.reshape(2, 4, gradient.shape[0] // 8, gradient.shape[1])


def quarters(value):
    return value.reshape(4, value.shape[0] // 4, value.shape[1])


def gather_x(value, x):
    cut = value.shape[0] // 2
    behind, ahead = move_x(value, 1), move_x(value, -1)
    far = jnp.concatenate([move_x(behind[:cut], 1), move_x(ahead[cut:], -1)])
    ring = jnp.stack([value, ahead, far, behind, value, ahead, far, behind])
    return lax.dynamic_slice_in_dim(ring, (4 - x) & 3, 4, 0)


def packed(value):
    return jnp.concatenate([value[:, k : k + 512] for k in range(0, value.shape[1], 512)])


def unpacked(rows, part, width):
    blocks = [rows[:, k * part : (k + 1) * part] for k in range(width // 512)]
    return jnp.concatenate(blocks, axis=2).reshape(4 * part, width)


def finish(values, x, core):
    sizes = [v.shape for v in values]
    together = gather_x(jnp.concatenate([packed(v) for v in values]), x)
    chips, at = [], 0
    for part, width in sizes:
        n = part * width // 512
        chip = unpacked(together[:, at : at + n], part, width)
        if width == 3072:
            blocks = chip.reshape(4, part, 4, width // 4).transpose(2, 1, 0, 3)
            chip = blocks.reshape(4 * part, width)
        chips.append(chip)
        at += n
    mine = [half_of(chip, core, 0) for chip in chips]
    theirs = [half_of(chip, 1 - core, 0) for chip in chips]
    arrived = swap_core(jnp.concatenate([packed(t) for t in theirs]))
    outs, at = [], 0
    for (part, width), own in zip(sizes, mine):
        n = 2 * part * width // 512
        rows = arrived[at : at + n]
        at += n
        other = jnp.concatenate(
            [rows[k * 2 * part : (k + 1) * 2 * part] for k in range(width // 512)], axis=1
        )
        outs.append((own.astype(f32), other.astype(f32)))
    return outs


def row_scale(values):
    return lax.rsqrt(jnp.mean(values * values, axis=-1, keepdims=True) + epsilon)


def rotation_tables(length):
    half_size = HEAD // 2
    places = jnp.arange(length, dtype=f32)
    frequencies = rope_base ** (-jnp.arange(half_size, dtype=f32) * 2.0 / HEAD)
    angles = places[:, None] * frequencies[None, :]
    cosine, sine = jnp.cos(angles), jnp.sin(angles)
    return jnp.concatenate([cosine, cosine], 1), jnp.concatenate([-sine, sine], 1)


def norm_backward(upstream, normed, scaling, gain_vector):
    gain_part = jnp.sum(upstream * normed, axis=tuple(range(upstream.ndim - 1)))
    scaled = upstream * gain_vector
    return (
        scaling * (scaled - normed * jnp.mean(scaled * normed, axis=-1, keepdims=True)),
        gain_part,
    )


def dot(left, right):
    return jnp.dot(left, right, preferred_element_type=f32)


def dot_t(left, right):
    return lax.dot_general(left, right, (((1,), (1,)), ((), ())), preferred_element_type=f32)


def dot_first(left, right):
    return lax.dot_general(left, right, (((0,), (0,)), ((), ())), preferred_element_type=f32)


def turned(values, cosine, sine):
    return values * cosine + pltpu.roll(values, HEAD // 2, 1) * sine


def scaled_heads(qkv, query_gain, key_gain, cosine, sine):
    q = jnp.concatenate([qkv[:, :HEAD], qkv[:, HEAD : 2 * HEAD]])
    k, v = qkv[:, 2 * HEAD : 3 * HEAD], qkv[:, 3 * HEAD :].astype(low)
    q_scale, k_scale = row_scale(q), row_scale(k)
    qn, kn = q * q_scale, k * k_scale
    cosine_two, sine_two = jnp.concatenate([cosine] * 2), jnp.concatenate([sine] * 2)
    qr = turned(qn * query_gain, cosine_two, sine_two).astype(low)
    kr = turned(kn * key_gain, cosine, sine).astype(low)
    return qr, kr, v, qn, kn, q_scale, k_scale


def soft_scores(qr, kr):
    scores = dot_t(qr, kr) * ROOT
    query = lax.broadcasted_iota(jnp.int32, scores.shape, 0) & 127
    key = lax.broadcasted_iota(jnp.int32, scores.shape, 1)
    scores = jnp.where(query >= key, scores, -1e30)
    p = jnp.exp(scores - jnp.max(scores, axis=-1, keepdims=True))
    return p / jnp.sum(p, axis=-1, keepdims=True)


def attention_kernel(first, *refs):
    if first:
        hidden, gain, qg, kg, cosine, sine, w, wo, out, a1, qkv_out, att_out = refs
    else:
        sofar, a1, qg, kg, cosine, sine, w, wo, out, qkv_out, att_out = refs

    @pl.when(pl.program_id(0) == 0)
    def _():
        if first:
            h = hidden[...]
            a1[...] = (h * row_scale(h) * gain[...]).astype(low)
            out[...] = h
        else:
            out[...] = sofar[...]

    qkv = dot(a1[...], w[...])
    qkv_out[...] = qkv
    for s in range(2):
        rows = slice(128 * s, 128 * s + 128)
        qr, kr, v, *_ = scaled_heads(qkv[rows], qg[...], kg[...], cosine[...], sine[...])
        att = dot(soft_scores(qr, kr).astype(low), v).astype(low)
        att_out[rows, :HEAD] = att[:128]
        att_out[rows, HEAD:] = att[128:]
    out[...] += dot(att_out[...], wo[...])


def whole(shape):
    return pl.BlockSpec(shape, lambda i: (0,) * len(shape))


def columns_at(rows, width):
    return pl.BlockSpec((rows, width), lambda i: (0, i))


def rows_at(rows, width, start):
    return pl.BlockSpec((rows, width), lambda i: (start + i, 0))


def shape_of(rows, width, kind):
    return jax.ShapeDtypeStruct((rows, width), kind)


def call(kernel, steps, ins, outs, waits=()):
    specs, values = [p[0] for p in ins], [p[1] for p in ins]
    specs += [pl.BlockSpec(memory_space=pl.ANY)] * len(waits)
    values += list(waits)

    def body(*refs):
        kernel(*refs[: len(ins)], *refs[len(ins) + len(waits) :])

    return pl.pallas_call(
        body,
        grid=(steps,),
        in_specs=specs,
        out_specs=[p[0] for p in outs],
        out_shape=[p[1] for p in outs],
        compiler_params=pltpu.CompilerParams(vmem_limit_bytes=28 * 2**20),
        cost_estimate=pl.CostEstimate(flops=2**20, bytes_accessed=2**16, transcendentals=0),
    )(*values)


BLOCK = (256, MODEL)


def attention_half(half, state, w_half, w_out, gains, tables, waits=()):
    mixer_gain, query_gain, key_gain, _ = gains
    head, table = whole((1, HEAD)), whole((128, HEAD))
    ins = [(whole(BLOCK), state[0])]
    ins.append((whole((1, MODEL)), mixer_gain[None]) if half == 0 else (whole(BLOCK), state[1]))
    ins += [(head, query_gain[None]), (head, key_gain[None]), (table, tables[0]), (table, tables[1])]
    ins += [(columns_at(MODEL, 512), w_half), (rows_at(256, MODEL, 4 * half), w_out)]
    outs = [(whole(BLOCK), shape_of(*BLOCK, f32))]
    if half == 0:
        outs.append((whole(BLOCK), shape_of(*BLOCK, low)))
    outs.append((columns_at(256, 512), shape_of(256, 2048, f32)))
    outs.append((columns_at(256, 256), shape_of(256, 1024, low)))
    return call(functools.partial(attention_kernel, half == 0), 4, ins, outs, waits)


def dense_kernel(first, *refs):
    if first:
        hidden, gain, w, wd, out, a2, gu_out, z_out = refs
    else:
        sofar, a2, w, wd, out, gu_out, z_out = refs

    @pl.when(pl.program_id(0) == 0)
    def _():
        if first:
            h = hidden[...]
            a2[...] = (h * row_scale(h) * gain[...]).astype(low)
            out[...] = h
        else:
            out[...] = sofar[...]

    gu = dot(a2[...], w[...])
    gu_out[...] = gu.astype(gu_out.dtype)
    gate, up = gu[:, :512], gu[:, 512:]
    z = (gate * jax.nn.sigmoid(gate) * up).astype(low)
    z_out[...] = z
    out[...] += dot(z, wd[...])


def dense_half(half, state, w_half, w_down, gains):
    ins = [(whole(BLOCK), state[0])]
    ins.append((whole((1, MODEL)), gains[3][None]) if half == 0 else (whole(BLOCK), state[1]))
    ins += [(columns_at(MODEL, 1024), w_half), (rows_at(512, MODEL, 3 * half), w_down)]
    outs = [(whole(BLOCK), shape_of(*BLOCK, f32))]
    if half == 0:
        outs.append((whole(BLOCK), shape_of(*BLOCK, low)))
    outs.append((columns_at(256, 1024), shape_of(256, 3072, f32)))
    outs.append((columns_at(256, 512), shape_of(256, 1536, low)))
    return call(functools.partial(dense_kernel, half == 0), 3, ins, outs)


def forward_mixer(hidden, w_qkv, w_out, gains, tables, between=None):
    part, a1, qkv_0, att_0 = attention_half(0, (hidden,), w_qkv[0], w_out, gains, tables)
    waits = between(part) if between is not None else ()
    after_mixer, qkv_1, att_1 = attention_half(1, (part, a1), w_qkv[1], w_out, gains, tables, waits)
    return after_mixer, (hidden, a1, (qkv_0, qkv_1), (att_0, att_1), after_mixer)


def forward_dense(after_mixer, w_gu, w_down, gains):
    part, a2, gu_0, z_0 = dense_half(0, (after_mixer,), w_gu[0], w_down, gains)
    out, gu_1, z_1 = dense_half(1, (part, a2), w_gu[1], w_down, gains)
    return out, (a2, (gu_0, gu_1), (z_0, z_1))


def forward(hidden, weights, gains, tables):
    w_qkv, w_out, w_gu, w_down = weights
    after_mixer, saved = forward_mixer(hidden, w_qkv, w_out, gains, tables)
    out, saved_dense = forward_dense(after_mixer, w_gu, w_down, gains)
    return out, saved + saved_dense


def dense_back_kernel(first, *refs):
    sofar, refs = (None, refs) if first else (refs[0], refs[1:])
    dm, wd, gu, w, dgu_out, da2 = refs

    @pl.when(pl.program_id(0) == 0)
    def _():
        da2[...] = jnp.zeros_like(da2) if first else sofar[...]

    dz = dot_t(dm[...], wd[...])
    gate, up = gu[:, :512], gu[:, 512:]
    sig = jax.nn.sigmoid(gate)
    dg = (dz * up * sig * (1.0 + gate * (1.0 - sig))).astype(low)
    du = (dz * (gate * sig)).astype(low)
    dgu_out[:, :512] = dg
    dgu_out[:, 512:] = du
    da2[...] += dot_t(dgu_out[...], w[...])


def dense_back_half(half, sofar, dm, gu, w_half, w_down):
    ins = [] if half == 1 else [(whole(BLOCK), sofar)]
    ins += [(whole(BLOCK), dm), (rows_at(512, MODEL, 3 * half), w_down)]
    ins += [(columns_at(256, 1024), gu), (columns_at(MODEL, 1024), w_half)]
    outs = [(columns_at(256, 1024), shape_of(256, 3072, low)), (whole(BLOCK), shape_of(*BLOCK, f32))]
    kernel = functools.partial(dense_back_kernel, half == 1)
    return call(kernel, 3, ins, outs)


def normed_back(upstream, normed, scale, gain):
    gain_part = jnp.sum(upstream * normed, axis=0, keepdims=True)
    scaled = upstream * gain
    return scale * (scaled - normed * jnp.mean(scaled * normed, axis=-1, keepdims=True)), gain_part


def attention_back_kernel(first, *refs):
    sofar, refs = (None, refs) if first else (refs[:3], refs[3:])
    dr, wo, qkv, qg, kg, cosine, sine, w, dqkv_out, da1, q_grad, k_grad = refs

    @pl.when(pl.program_id(0) == 0)
    def _():
        for k, ref in enumerate((da1, q_grad, k_grad)):
            ref[...] = jnp.zeros_like(ref) if first else sofar[k][...]

    datt = dot_t(dr[...], wo[...]).astype(low)
    for s in range(2):
        rows = slice(128 * s, 128 * s + 128)
        cos, sin = cosine[...], sine[...]
        qr, kr, v, qn, kn, q_scale, k_scale = scaled_heads(qkv[rows, :], qg[...], kg[...], cos, sin)
        p = soft_scores(qr, kr)
        do = jnp.concatenate([datt[rows, :HEAD], datt[rows, HEAD:]])
        dp = dot_t(do, v)
        dv = dot_first(p.astype(low), do)
        ds = (p * (dp - jnp.sum(dp * p, axis=-1, keepdims=True))).astype(low)
        dqr, dkr = dot(ds, kr) * ROOT, dot_first(ds, qr) * ROOT
        cos_two, sin_two = jnp.concatenate([cos] * 2), jnp.concatenate([sin] * 2)
        dq, q_part = normed_back(turned(dqr, cos_two, -sin_two), qn, q_scale, qg[...])
        dk, k_part = normed_back(turned(dkr, cos, -sin), kn, k_scale, kg[...])
        q_grad[...] += q_part
        k_grad[...] += k_part
        dq = dq.astype(low)
        dqkv_out[rows, :HEAD] = dq[:128]
        dqkv_out[rows, HEAD : 2 * HEAD] = dq[128:]
        dqkv_out[rows, 2 * HEAD : 3 * HEAD] = dk.astype(low)
        dqkv_out[rows, 3 * HEAD :] = dv.astype(low)
    da1[...] += dot_t(dqkv_out[...], w[...])


def attention_back_half(half, sofar, dr, qkv, w_half, w_out, gains, tables, waits=()):
    head, table = whole((1, HEAD)), whole((128, HEAD))
    ins = [] if half == 1 else [(whole(BLOCK), sofar[0]), (head, sofar[1]), (head, sofar[2])]
    ins += [(whole(BLOCK), dr), (rows_at(256, MODEL, 4 * half), w_out), (columns_at(256, 512), qkv)]
    ins += [(head, gains[1][None]), (head, gains[2][None]), (table, tables[0]), (table, tables[1])]
    ins += [(columns_at(MODEL, 512), w_half)]
    outs = [(columns_at(256, 512), shape_of(256, 2048, low)), (whole(BLOCK), shape_of(*BLOCK, f32))]
    outs += [(head, shape_of(1, HEAD, f32))] * 2
    kernel = functools.partial(attention_back_kernel, half == 1)
    return call(kernel, 4, ins, outs, waits)


def backward(cotangent, saved, weights, gains, tables, between=None):
    w_qkv, w_out, w_gu, w_down = weights
    mixer_gain, query_gain, key_gain, dense_gain = gains
    hidden, a1, qkv, att, after_mixer, a2, gu, z = saved
    dm = cotangent.astype(low)
    dgu_1, da2 = dense_back_half(1, None, dm, gu[1], w_gu[1], w_down)
    dgu_0, da2 = dense_back_half(0, da2, dm, gu[0], w_gu[0], w_down)
    if between is not None:
        da2 = between[0]((dgu_0, dgu_1), da2)
    scale_two = row_scale(after_mixer)
    part, dense_gain_grad = norm_backward(da2, after_mixer * scale_two, scale_two, dense_gain)
    dh2 = cotangent + part
    dr = dh2.astype(low)
    g_out = None
    if between is not None:
        dr, g_out = between[1](dr)
    dqkv_1, *so_far = attention_back_half(1, None, dr, qkv[1], w_qkv[1], w_out, gains, tables)
    if between is not None:
        dr = between[3](dr, dqkv_1, g_out)
    dqkv_0, da1, q_grad, k_grad = attention_back_half(
        0, so_far, dr, qkv[0], w_qkv[0], w_out, gains, tables
    )
    if between is not None:
        da1 = between[2]((dqkv_0, dqkv_1), da1, g_out)
    scale_one = row_scale(hidden)
    part, mixer_gain_grad = norm_backward(da1, hidden * scale_one, scale_one, mixer_gain)
    dh = dh2 + part
    return dh, (mixer_gain_grad, dense_gain_grad, q_grad[0], k_grad[0])


def product(left, left_other, right, right_other):
    both_left = jnp.concatenate([left, left_other])
    both_right = jnp.concatenate([right, right_other])
    dims = (((0,), (0,)), ((), ()))
    return lax.dot_general(both_left, both_right, dims, preferred_element_type=f32).astype(low)


def on_device(
    boundary,
    mixer_gain,
    query_weight,
    key_weight,
    value_weight,
    output_weight,
    query_gain,
    key_gain,
    dense_gain,
    gate_weight,
    up_weight,
    down_weight,
):
    first_section = lax.axis_index("section") == 0
    x = lax.axis_index("dp")
    place_at = lax.axis_index("fsdp")
    core, y, z = place_at & 1, (place_at >> 1) & 3, place_at >> 3
    spot = (x, z, y)
    local = boundary[0, :, 0].astype(f32).reshape(256, MODEL)

    gain_tile = jnp.stack(
        [mixer_gain[0], dense_gain[0], jnp.pad(query_gain[0], (0, 56)), jnp.pad(key_gain[0], (0, 56))],
        axis=1,
    )
    gain_tile = jnp.pad(gain_tile, ((0, 0), (0, 124)))

    shards = (query_weight, key_weight, value_weight, output_weight)
    shards += (gate_weight, up_weight, down_weight)
    kept, sent = pack_halves([shard[0] for shard in shards], gain_tile, core)
    chip = in_order(kept, swap_core(sent), core, 0)
    zero = jnp.zeros_like(z)
    z_own = z ^ core

    with jax.named_scope("ag_dense"):
        d_0 = lax.dynamic_slice(chip, (x * 32, zero + 3200), (32, 4608))
        d_z = swap_z(d_0)
        d_pair = jnp.stack([d_0, d_z])
        d_near = near_y(d_pair)
        m_0 = chip[:, :3200]
        m_z = swap_z(m_0)
        d_near, m_z = tied(d_near, m_z)
        d_far = far_y(*d_near)
        d_all = (jnp.concatenate([d_pair, d_near[0]]), jnp.concatenate([d_near[1], *d_far]))
        d_x = near_x(*d_all)
    with jax.named_scope("ag_mixer"):
        m_pair = jnp.stack([m_0, m_z])
        m_near = near_y(m_pair)
        m_near, d_x = tied(m_near, d_x)
        m_far = far_y(*m_near)
        moves, offsets = [], []
        spots = [(0, 0), (0, 1), (1, 0), (1, 1), (2, 0), (2, 1), (3, 0), (4, 0)]
        for (piece, index), (dz, dy) in zip(spots, origins):
            moves.append((piece, index, 0, 0, 128, 2176, 0))
            offsets.append(((z ^ dz) * 4 + ((y - dy) & 3)) * 128)
            block = ((z_own ^ dz) * 4 + ((y - dy) & 3)) * 256
            for k in range(2):
                for m in range(2):
                    moves.append((piece, index, 64 * k, 2176 + 512 * m, 64, 512, 1))
                    offsets.append(block + 128 * k + 64 * m)
        own_qkv, own_out = place(
            (m_pair, *m_near, *m_far), moves, offsets, ((MODEL, 2176), (2048, 512))
        )
        w_qkv = (own_qkv, swap_core(own_qkv))
        w_out = joined(own_out, core)
    tile = own_qkv[:, 2048:2052].astype(f32)
    gains = (
        tile[:, 0],
        tile[:, 2].reshape(16, 64)[:, :8].reshape(HEAD),
        tile[:, 3].reshape(16, 64)[:, :8].reshape(HEAD),
        tile[:, 1],
    )
    tables = rotation_tables(128)
    d_x_far = far_x(*d_x)

    def place_dense(part):
        moves, offsets = [], []
        for piece, dx in enumerate((0, 0, 1, 1, 3, 3, 2, 2)):
            turn = (x - dx) & 3
            for index, n in enumerate(range(4 * (piece & 1), 4 * (piece & 1) + 4)):
                dz, dy = origins[n]
                moves.append((piece, index, 0, 0, 32, 3072, 0))
                offsets.append(((z ^ dz) * 4 + ((y - dy) & 3)) * 128 + turn * 32)
                block = ((z_own ^ dz) * 4 + ((y - dy) & 3)) * 384 + (turn >> 1) * 192
                for m in range(3):
                    moves.append((piece, index, 0, 3072 + 512 * m, 32, 512, 1))
                    offsets.append(block + 64 * m + (turn & 1) * 32)
        return place((*d_all, *d_x, *d_x_far), moves, offsets, ((MODEL, 3072), (3072, 512)), (part, w_qkv[1]))

    own_dense = []

    def between_halves(part):
        own_dense.extend(place_dense(part))
        return (own_dense[0],)

    with jax.named_scope("f1"):
        early_mixer, _ = forward_mixer(local, w_qkv, w_out, gains, tables, between_halves)
    with jax.named_scope("ag_dense"):
        own_gu, own_down = own_dense
        w_gu = (own_gu, swap_core(own_gu))
        w_down = joined(own_down, core)
    weights = (w_qkv, w_out, w_gu, w_down)
    with jax.named_scope("f1"):
        early, _ = forward_dense(early_mixer, w_gu, w_down, gains)
    arrived = move_section(early.astype(low), 1).astype(f32)
    with jax.named_scope("f2"):
        out, saved = forward(jnp.where(first_section, local, arrived), weights, gains, tables)
    _, a1, _, att, _, a2, _, z_low = saved
    with jax.named_scope("b1"):
        early_dh, _ = backward(local, saved, weights, gains, tables)
    returned = move_section(early_dh.astype(low), -1).astype(f32)
    cotangent = jnp.where(first_section, returned, local)

    acts = jnp.concatenate([a1, att[1], att[0], a2, z_low[1], z_low[0]], axis=1)
    acts = swap_core(acts)
    a1_o, att_o = acts[:, :1024], (acts[:, 1024:2048], acts[:, 2048:3072])
    a2_o, z_o = acts[:, 3072:4096], (acts[:, 4096:5632], acts[:, 5632:])

    def by_halves(left, left_other, right, right_other):
        parts = [product(a, b, right, right_other) for a, b in zip(left, left_other)]
        return by_chip(jnp.concatenate(parts))

    cot_mine, cot_theirs = half_of(cotangent, core, 1), half_of(cotangent, 1 - core, 1)
    z_flip = z ^ core
    done = {}

    def after_dgu(dgu, da2):
        with jax.named_scope("g_gu"):
            g_gu = product(a2, a2_o, dgu[0], swap_core(dgu[1])).reshape(8, 128, 3072)
            da2, g_gu = tied(da2, g_gu)

            def columns_of(place, start=0, width=768):
                return lax.dynamic_slice_in_dim(g_gu, place * 768 + start, width, 2)

            done["gu"] = (columns_of, reduce_x_first(columns_of, x))
        with jax.named_scope("g_down"):
            dm_o = swap_core(cot_theirs.astype(low))
            g_down = by_halves(z_low, z_o, cot_mine.astype(low), dm_o)
            da2, g_down = tied(da2, g_down)
            done["down"] = g_down
        return da2

    def after_dr(dr):
        with jax.named_scope("g_out"):
            dr_o = swap_core(half_of(dr, 1 - core, 1))
            g_out = by_halves(att, att_o, half_of(dr, core, 1), dr_o)
            g_do = jnp.concatenate([done["down"], g_out], axis=2)
            dr, g_do = tied(dr, g_do)
        with jax.named_scope("rs_do"):
            done["do"] = reduce_y_first(g_do, z_flip, y)
        return dr, g_do

    def between_heads(dr, dqkv_1, g_do):
        first_x, first_y, dqkv_1 = tied(done["gu"][1], done["do"], dqkv_1)
        with jax.named_scope("g_qkv"):
            done["dqkv_o"] = swap_core(dqkv_1)
        ready = []
        with jax.named_scope("rs_gu"):
            ready.append(reduce_x_ready(done["gu"][0], x, first_x))
        with jax.named_scope("rs_do"):
            ready.append(reduce_y_ready(g_do, z_flip, y, first_y))
        dr, ready = tied(dr, ready)
        with jax.named_scope("rs_gu"):
            done["gu2"] = near_x_two(*ready[0])
        with jax.named_scope("rs_do"):
            done["do2"] = near_y_two(*ready[1])
        return dr

    def after_attention(dqkv, da1, g_do):
        own = dqkv[0]
        with jax.named_scope("g_qkv"):
            g_qkv = by_chip(product(a1, a1_o, own, done["dqkv_o"]))
            da1, g_qkv = tied(da1, g_qkv)
        with jax.named_scope("rs_q"):
            first = reduce_y_first(g_qkv, z, y)
        first, second = tied(first, done["do2"])
        with jax.named_scope("rs_q"):
            done["q"] = (g_qkv, reduce_y_second(g_qkv, z, y, first))
        with jax.named_scope("rs_gu"):
            mine = reduce_x_third(done["gu"][0], x, done["gu2"]).reshape(2, 4, 128, 768)
            done["g"] = (mine, reduce_y_first(mine, z, y))
        with jax.named_scope("rs_do"):
            done["s_do"] = added(*reduce_z(g_do, z_flip, y, second))
        return da1

    with jax.named_scope("b2"):
        dh, gain_grads = backward(
            cotangent, saved, weights, gains, tables, (after_dgu, after_dr, after_attention, between_heads)
        )
    endpoints = jnp.where(first_section, dh, out).reshape(1, 2, 1, 128, MODEL)
    g_qkv, q_second = done["q"]
    mine, g_first = done["g"]
    gain_part = jnp.concatenate(gain_grads).reshape(18, 128)
    mine, gain_part = tied(mine, gain_part)
    gain_part = summed_over(summed_x(gain_part), 1, 8)
    q_second, g_first = tied(q_second, g_first)
    with jax.named_scope("rs_gu"):
        g_second = reduce_y_second(mine, z, y, g_first)
    with jax.named_scope("rs_q"):
        q_z = reduce_z(g_qkv, z, y, q_second)
        q_z, g_second = tied(q_z, g_second)
        s_q = added(*q_z)
    with jax.named_scope("rs_gu"):
        s_gu = added(*reduce_z(mine, z, y, g_second))
    with jax.named_scope("rs_x"):
        s_do, s_qkv = quarters(done["s_do"][:384]), quarters(s_q)
        s_o = quarters(done["s_do"][384:])
        blocks = [s_qkv[:, :, k : k + 512] for k in range(0, 2048, 512)] + [s_do, s_o]
        mine = reduce_x(jnp.concatenate(blocks, axis=1), x)
        m_qkv = jnp.concatenate([mine[k : k + 32] for k in range(0, 128, 32)], axis=1)
        m_gu = jnp.concatenate([s_gu[k : k + 32] for k in range(0, 128, 32)], axis=1)
    with jax.named_scope("fin"):
        parts = (m_qkv, m_gu, mine[128:224], mine[224:])
        qkv, gu, down, out_w = finish(parts, x, core)

    def both(pair, start, width, block=None):
        block = block or pair[0].shape[1]

        def part(value):
            starts = range(start, value.shape[1], block)
            return jnp.concatenate([value[:, k : k + width] for k in starts], axis=1)

        return in_order(*(part(p) for p in pair), core, 1)[None]

    sums = summed_over(gain_part, 2, 4).reshape(-1)

    def gain_rows(start, width):
        return lax.dynamic_slice_in_dim(sums, start + place_at * width, width, 0)[None]

    return (
        endpoints,
        gain_rows(0, 64),
        both(qkv, 0, 256, 512),
        both(qkv, 256, 128, 512),
        both(qkv, 384, 128, 512),
        both(out_w, 0, 512),
        gain_rows(2048, 8),
        gain_rows(2176, 8),
        gain_rows(1024, 64),
        both(gu, 0, 512, 1024),
        both(gu, 512, 512, 1024),
        both(down, 0, 512),
    )


def solution(mesh):
    placed = (
        P("section", None, ("dp", "fsdp"), None, None),
        P("section", "fsdp"),
        P("section", "fsdp", None),
        P("section", "fsdp", None),
        P("section", "fsdp", None),
        P("section", "fsdp", None),
        P("section", "fsdp"),
        P("section", "fsdp"),
        P("section", "fsdp"),
        P("section", "fsdp", None),
        P("section", "fsdp", None),
        P("section", "fsdp", None),
    )
    return jax.shard_map(
        on_device,
        mesh=mesh,
        in_specs=placed,
        out_specs=(
            P("section", None, ("dp", "fsdp"), None, None),
            P("section", "fsdp"),
            P("section", "fsdp", None),
            P("section", "fsdp", None),
            P("section", "fsdp", None),
            P("section", "fsdp", None),
            P("section", "fsdp"),
            P("section", "fsdp"),
            P("section", "fsdp"),
            P("section", "fsdp", None),
            P("section", "fsdp", None),
            P("section", "fsdp", None),
        ),
        check_vma=False,
    )
```

```python
import functools

import jax
import jax.numpy as jnp
from jax import lax
from jax.experimental import pallas as pl
from jax.experimental.pallas import tpu as pltpu
from jax.sharding import PartitionSpec as P

epsilon = 1e-06
rope_base = 1000000.0
low = jnp.bfloat16
f32 = jnp.float32
MODEL = 1024
HEAD = 128
ROOT = HEAD ** (-0.5)


def tied(*values):
    return lax.optimization_barrier(values)


def swap_core(value):
    return lax.ppermute(value, "fsdp", [(i, i ^ 1) for i in range(16)])


def swap_z(value):
    return lax.ppermute(value, "fsdp", [(i, i ^ 8) for i in range(16)])


def move_y(value, step):
    pairs = [(i, (i & 8) | ((((i >> 1) + step) & 3) << 1) | (i & 1)) for i in range(16)]
    return lax.ppermute(value, "fsdp", pairs)


def move_x(value, step):
    return lax.ppermute(value, "dp", [(i, (i + step) % 4) for i in range(4)])


def move_section(value, step):
    return lax.ppermute(value, "section", [(0, 1)] if step > 0 else [(1, 0)])


def summed_x(value):
    for step in (1, 2):
        value = value + lax.ppermute(value, "dp", [(i, i ^ step) for i in range(4)])
    return value


def summed_over(value, *steps):
    for step in steps:
        value = value + lax.ppermute(value, "fsdp", [(i, i ^ step) for i in range(16)])
    return value


def pick(value, *where):
    start = list(where) + [0] * (value.ndim - len(where))
    size = [1] * len(where) + list(value.shape[len(where) :])
    return lax.dynamic_slice(value, start, size).reshape(value.shape[len(where) :])


def half_of(value, index, axis):
    width = value.shape[axis] // 2
    return lax.dynamic_slice_in_dim(value, index * width, width, axis)


def in_order(own, other, core, axis):
    first = jnp.where(core == 0, own, other)
    second = jnp.where(core == 0, other, own)
    return jnp.concatenate([first, second], axis=axis)


def placing_kernel(moves, sources_count, skipped, offsets, *refs):
    sources, outs, sems = refs[:sources_count], refs[sources_count + skipped : -1], refs[-1]
    copies = []
    for n, (source, index, row, column, rows, width, out) in enumerate(moves):
        block = sources[source].at[index, pl.ds(row, rows), pl.ds(column, width)]
        at = pl.multiple_of(offsets[n], 16)
        copies.append(pltpu.make_async_copy(block, outs[out].at[pl.ds(at, rows)], sems.at[n]))
    for copy in copies:
        copy.start()
    for copy in copies:
        copy.wait()


def place(pieces, moves, offsets, shapes, waits=()):
    return pl.pallas_call(
        functools.partial(placing_kernel, tuple(moves), len(pieces), len(waits)),
        out_shape=[jax.ShapeDtypeStruct(shape, low) for shape in shapes],
        in_specs=[pl.BlockSpec(memory_space=pltpu.SMEM)]
        + [pl.BlockSpec(memory_space=pl.ANY)] * (len(pieces) + len(waits)),
        out_specs=[pl.BlockSpec(memory_space=pltpu.VMEM)] * len(shapes),
        scratch_shapes=[pltpu.SemaphoreType.DMA((len(moves),))],
        compiler_params=pltpu.CompilerParams(vmem_limit_bytes=16 * 2**20),
        cost_estimate=pl.CostEstimate(flops=2**20, bytes_accessed=2**16, transcendentals=0),
    )(jnp.stack(offsets).astype(jnp.int32), *pieces, *waits)


def packing_kernel(moves, count, core_ref, *refs):
    sources, outs, sems = refs[:count], refs[count:-1], refs[-1]
    copies = []
    for k, out in enumerate(outs):
        half = core_ref[0] if k == 0 else 1 - core_ref[0]
        for n, (source, row, half_width, column, width, at) in enumerate(moves):
            start = pl.multiple_of(half * half_width + column, 128)
            block = sources[source].at[pl.ds(row, 64), pl.ds(start, width)]
            sem = sems.at[k * len(moves) + n]
            copies.append(pltpu.make_async_copy(block, out.at[:, pl.ds(at, width)], sem))
    for copy in copies:
        copy.start()
    for copy in copies:
        copy.wait()


def pack_halves(weights, gain_tile, core):
    q, k, v, out, gate, up, down = weights
    moves = []
    for b in range(4):
        moves += [(0, 0, 1024, 256 * b, 256), (1, 0, 512, 128 * b, 128), (2, 0, 512, 128 * b, 128)]
    moves.append((7, 0, 0, 0, 128))
    moves += [(3, 64 * m, 512, 0, 512) for m in range(2)]
    for b in range(3):
        moves += [(4, 0, 1536, 512 * b, 512), (5, 0, 1536, 512 * b, 512)]
    moves += [(6, 64 * m, 512, 0, 512) for m in range(3)]
    at, placed = 0, []
    for move in moves:
        placed.append((*move, at))
        at += move[-1]
    shape = jax.ShapeDtypeStruct((64, at), low)
    return pl.pallas_call(
        functools.partial(packing_kernel, tuple(placed), 8),
        out_shape=[shape, shape],
        in_specs=[pl.BlockSpec(memory_space=pltpu.SMEM)] + [pl.BlockSpec(memory_space=pl.ANY)] * 8,
        out_specs=[pl.BlockSpec(memory_space=pltpu.VMEM)] * 2,
        scratch_shapes=[pltpu.SemaphoreType.DMA((2 * len(placed),))],
        compiler_params=pltpu.CompilerParams(vmem_limit_bytes=8 * 2**20),
    )(core.reshape(1).astype(jnp.int32), q, k, v, out, gate, up, down, gain_tile)


def joining_kernel(core_ref, own, other, out, sems):
    rows, width = own.shape
    cut = rows // 2
    mine = pl.multiple_of(core_ref[0] * width, width)
    theirs = pl.multiple_of((1 - core_ref[0]) * width, width)
    upper, lower = pl.ds(0, cut), pl.ds(cut, cut)
    copies = (
        pltpu.make_async_copy(own, out.at[:, pl.ds(mine, width)], sems.at[0]),
        pltpu.make_async_copy(other.at[lower], out.at[upper, pl.ds(theirs, width)], sems.at[1]),
        pltpu.make_async_copy(other.at[upper], out.at[lower, pl.ds(theirs, width)], sems.at[2]),
    )
    for copy in copies:
        copy.start()
    for copy in copies:
        copy.wait()


def joined(own, core):
    rows, width = own.shape
    return pl.pallas_call(
        joining_kernel,
        out_shape=jax.ShapeDtypeStruct((rows, 2 * width), low),
        in_specs=[pl.BlockSpec(memory_space=pltpu.SMEM)] + [pl.BlockSpec(memory_space=pl.ANY)] * 2,
        out_specs=pl.BlockSpec(memory_space=pltpu.VMEM),
        scratch_shapes=[pltpu.SemaphoreType.DMA((3,))],
        compiler_params=pltpu.CompilerParams(vmem_limit_bytes=16 * 2**20),
        cost_estimate=pl.CostEstimate(flops=2**20, bytes_accessed=2**16, transcendentals=0),
    )(core.reshape(1).astype(jnp.int32), own, swap_core(own))


origins = [(0, 0), (1, 0), (0, 1), (1, 1), (0, 3), (1, 3), (0, 2), (1, 2)]


def near_y(pair):
    return move_y(pair, 1), move_y(pair, -1)


def far_y(behind, ahead):
    return move_y(behind[0], 1)[None], move_y(ahead[1], -1)[None]


def near_x(first, second):
    return move_x(first, 1), move_x(second, 1), move_x(first, -1), move_x(second, -1)


def far_x(behind_first, behind_second, ahead_first, ahead_second):
    return move_x(behind_first, 1), move_x(ahead_second, -1)


def added(left, right):
    return (left.astype(f32) + right.astype(f32)).astype(low)


def reduce_x_first(take, x):
    far = take((x + 2) & 3)
    cut = far.shape[0] // 2
    return move_x(far[:cut], 1), move_x(far[cut:], -1)


def reduce_x_ready(take, x, first):
    up, down = first
    cut = up.shape[0]
    after_it, before = take((x + 1) & 3), take((x - 1) & 3)
    after_it = jnp.concatenate([added(after_it[:cut], up), after_it[cut:]])
    before = jnp.concatenate([before[:cut], added(before[cut:], down)])
    return after_it, before


def reduce_x_third(take, x, second):
    own = take(x)
    return (own.astype(f32) + second[0].astype(f32) + second[1].astype(f32)).astype(low)


def reduce_x(values, x):
    def take(place):
        return pick(values, place)

    second = near_x_two(*reduce_x_ready(take, x, reduce_x_first(take, x)))
    return reduce_x_third(take, x, second)


def near_x_two(up, down):
    return move_x(up, 1), move_x(down, -1)


def near_y_two(up, down):
    return move_y(up, 1), move_y(down, -1)


def reduce_y_first(values, z, y):
    far = (y + 2) & 3
    return move_y(pick(values, z, far), 1), move_y(pick(values, 1 - z, far), -1)


def reduce_y_ready(values, z, y, first):
    up, down = first
    other, y_after, y_before = 1 - z, (y + 1) & 3, (y - 1) & 3
    after_it = jnp.stack([added(pick(values, z, y_after), up), pick(values, other, y_after)])
    before = jnp.stack([pick(values, z, y_before), added(pick(values, other, y_before), down)])
    return after_it, before


def reduce_y_second(values, z, y, first):
    return near_y_two(*reduce_y_ready(values, z, y, first))


def reduce_z(values, z, y, second):
    def total(k, zi):
        own = pick(values, zi, y)
        return (own.astype(f32) + second[0][k].astype(f32) + second[1][k].astype(f32)).astype(low)

    return total(0, z), swap_z(total(1, 1 - z))


def by_chip(gradient):
    return gradient.reshape(2, 4, gradient.shape[0] // 8, gradient.shape[1])


def quarters(value):
    return value.reshape(4, value.shape[0] // 4, value.shape[1])


def gather_x(value, x):
    cut = value.shape[0] // 2
    behind, ahead = move_x(value, 1), move_x(value, -1)
    far = jnp.concatenate([move_x(behind[:cut], 1), move_x(ahead[cut:], -1)])
    ring = jnp.stack([value, ahead, far, behind, value, ahead, far, behind])
    return lax.dynamic_slice_in_dim(ring, (4 - x) & 3, 4, 0)


def packed(value):
    return jnp.concatenate([value[:, k : k + 512] for k in range(0, value.shape[1], 512)])


def unpacked(rows, part, width):
    blocks = [rows[:, k * part : (k + 1) * part] for k in range(width // 512)]
    return jnp.concatenate(blocks, axis=2).reshape(4 * part, width)


def finish(values, x, core):
    sizes = [v.shape for v in values]
    together = gather_x(jnp.concatenate([packed(v) for v in values]), x)
    chips, at = [], 0
    for part, width in sizes:
        n = part * width // 512
        chip = unpacked(together[:, at : at + n], part, width)
        if width == 3072:
            blocks = chip.reshape(4, part, 4, width // 4).transpose(2, 1, 0, 3)
            chip = blocks.reshape(4 * part, width)
        chips.append(chip)
        at += n
    mine = [half_of(chip, core, 0) for chip in chips]
    theirs = [half_of(chip, 1 - core, 0) for chip in chips]
    arrived = swap_core(jnp.concatenate([packed(t) for t in theirs]))
    outs, at = [], 0
    for (part, width), own in zip(sizes, mine):
        n = 2 * part * width // 512
        rows = arrived[at : at + n]
        at += n
        other = jnp.concatenate(
            [rows[k * 2 * part : (k + 1) * 2 * part] for k in range(width // 512)], axis=1
        )
        outs.append((own.astype(f32), other.astype(f32)))
    return outs


def row_scale(values):
    return lax.rsqrt(jnp.mean(values * values, axis=-1, keepdims=True) + epsilon)


def rotation_tables(length):
    half_size = HEAD // 2
    places = jnp.arange(length, dtype=f32)
    frequencies = rope_base ** (-jnp.arange(half_size, dtype=f32) * 2.0 / HEAD)
    angles = places[:, None] * frequencies[None, :]
    cosine, sine = jnp.cos(angles), jnp.sin(angles)
    return jnp.concatenate([cosine, cosine], 1), jnp.concatenate([-sine, sine], 1)


def norm_backward(upstream, normed, scaling, gain_vector):
    gain_part = jnp.sum(upstream * normed, axis=tuple(range(upstream.ndim - 1)))
    scaled = upstream * gain_vector
    return (
        scaling * (scaled - normed * jnp.mean(scaled * normed, axis=-1, keepdims=True)),
        gain_part,
    )


def dot(left, right):
    return jnp.dot(left, right, preferred_element_type=f32)


def dot_t(left, right):
    return lax.dot_general(left, right, (((1,), (1,)), ((), ())), preferred_element_type=f32)


def dot_first(left, right):
    return lax.dot_general(left, right, (((0,), (0,)), ((), ())), preferred_element_type=f32)


def turned(values, cosine, sine):
    return values * cosine + pltpu.roll(values, HEAD // 2, 1) * sine


def scaled_heads(qkv, query_gain, key_gain, cosine, sine):
    q = jnp.concatenate([qkv[:, :HEAD], qkv[:, HEAD : 2 * HEAD]])
    k, v = qkv[:, 2 * HEAD : 3 * HEAD], qkv[:, 3 * HEAD :].astype(low)
    q_scale, k_scale = row_scale(q), row_scale(k)
    qn, kn = q * q_scale, k * k_scale
    cosine_two, sine_two = jnp.concatenate([cosine] * 2), jnp.concatenate([sine] * 2)
    qr = turned(qn * query_gain, cosine_two, sine_two).astype(low)
    kr = turned(kn * key_gain, cosine, sine).astype(low)
    return qr, kr, v, qn, kn, q_scale, k_scale


def soft_scores(qr, kr):
    scores = dot_t(qr, kr) * ROOT
    query = lax.broadcasted_iota(jnp.int32, scores.shape, 0) & 127
    key = lax.broadcasted_iota(jnp.int32, scores.shape, 1)
    scores = jnp.where(query >= key, scores, -1e30)
    p = jnp.exp(scores - jnp.max(scores, axis=-1, keepdims=True))
    return p / jnp.sum(p, axis=-1, keepdims=True)


def attention_kernel(first, *refs):
    if first:
        hidden, gain, qg, kg, cosine, sine, w, wo, out, a1, qkv_out, att_out = refs
    else:
        sofar, a1, qg, kg, cosine, sine, w, wo, out, qkv_out, att_out = refs

    @pl.when(pl.program_id(0) == 0)
    def _():
        if first:
            h = hidden[...]
            a1[...] = (h * row_scale(h) * gain[...]).astype(low)
            out[...] = h
        else:
            out[...] = sofar[...]

    qkv = dot(a1[...], w[...])
    qkv_out[...] = qkv
    for s in range(2):
        rows = slice(128 * s, 128 * s + 128)
        qr, kr, v, *_ = scaled_heads(qkv[rows], qg[...], kg[...], cosine[...], sine[...])
        att = dot(soft_scores(qr, kr).astype(low), v).astype(low)
        att_out[rows, :HEAD] = att[:128]
        att_out[rows, HEAD:] = att[128:]
    out[...] += dot(att_out[...], wo[...])


def whole(shape):
    return pl.BlockSpec(shape, lambda i: (0,) * len(shape))


def columns_at(rows, width):
    return pl.BlockSpec((rows, width), lambda i: (0, i))


def rows_at(rows, width, start):
    return pl.BlockSpec((rows, width), lambda i: (start + i, 0))


def shape_of(rows, width, kind):
    return jax.ShapeDtypeStruct((rows, width), kind)


def call(kernel, steps, ins, outs, waits=()):
    specs, values = [p[0] for p in ins], [p[1] for p in ins]
    specs += [pl.BlockSpec(memory_space=pl.ANY)] * len(waits)
    values += list(waits)

    def body(*refs):
        kernel(*refs[: len(ins)], *refs[len(ins) + len(waits) :])

    return pl.pallas_call(
        body,
        grid=(steps,),
        in_specs=specs,
        out_specs=[p[0] for p in outs],
        out_shape=[p[1] for p in outs],
        compiler_params=pltpu.CompilerParams(vmem_limit_bytes=28 * 2**20),
        cost_estimate=pl.CostEstimate(flops=2**20, bytes_accessed=2**16, transcendentals=0),
    )(*values)


BLOCK = (256, MODEL)


def attention_half(half, state, w_half, w_out, gains, tables, waits=()):
    mixer_gain, query_gain, key_gain, _ = gains
    head, table = whole((1, HEAD)), whole((128, HEAD))
    ins = [(whole(BLOCK), state[0])]
    ins.append((whole((1, MODEL)), mixer_gain[None]) if half == 0 else (whole(BLOCK), state[1]))
    ins += [(head, query_gain[None]), (head, key_gain[None]), (table, tables[0]), (table, tables[1])]
    ins += [(columns_at(MODEL, 512), w_half), (rows_at(256, MODEL, 4 * half), w_out)]
    outs = [(whole(BLOCK), shape_of(*BLOCK, f32))]
    if half == 0:
        outs.append((whole(BLOCK), shape_of(*BLOCK, low)))
    outs.append((columns_at(256, 512), shape_of(256, 2048, f32)))
    outs.append((columns_at(256, 256), shape_of(256, 1024, low)))
    return call(functools.partial(attention_kernel, half == 0), 4, ins, outs, waits)


def dense_kernel(first, *refs):
    if first:
        hidden, gain, w, wd, out, a2, gu_out, z_out = refs
    else:
        sofar, a2, w, wd, out, gu_out, z_out = refs

    @pl.when(pl.program_id(0) == 0)
    def _():
        if first:
            h = hidden[...]
            a2[...] = (h * row_scale(h) * gain[...]).astype(low)
            out[...] = h
        else:
            out[...] = sofar[...]

    gu = dot(a2[...], w[...])
    gu_out[...] = gu.astype(gu_out.dtype)
    gate, up = gu[:, :512], gu[:, 512:]
    z = (gate * jax.nn.sigmoid(gate) * up).astype(low)
    z_out[...] = z
    out[...] += dot(z, wd[...])


def dense_half(half, state, w_half, w_down, gains):
    ins = [(whole(BLOCK), state[0])]
    ins.append((whole((1, MODEL)), gains[3][None]) if half == 0 else (whole(BLOCK), state[1]))
    ins += [(columns_at(MODEL, 1024), w_half), (rows_at(512, MODEL, 3 * half), w_down)]
    outs = [(whole(BLOCK), shape_of(*BLOCK, f32))]
    if half == 0:
        outs.append((whole(BLOCK), shape_of(*BLOCK, low)))
    outs.append((columns_at(256, 1024), shape_of(256, 3072, f32)))
    outs.append((columns_at(256, 512), shape_of(256, 1536, low)))
    return call(functools.partial(dense_kernel, half == 0), 3, ins, outs)


def forward_mixer(hidden, w_qkv, w_out, gains, tables, between=None):
    part, a1, qkv_0, att_0 = attention_half(0, (hidden,), w_qkv[0], w_out, gains, tables)
    waits = between(part) if between is not None else ()
    after_mixer, qkv_1, att_1 = attention_half(1, (part, a1), w_qkv[1], w_out, gains, tables, waits)
    return after_mixer, (hidden, a1, (qkv_0, qkv_1), (att_0, att_1), after_mixer)


def forward_dense(after_mixer, w_gu, w_down, gains):
    part, a2, gu_0, z_0 = dense_half(0, (after_mixer,), w_gu[0], w_down, gains)
    out, gu_1, z_1 = dense_half(1, (part, a2), w_gu[1], w_down, gains)
    return out, (a2, (gu_0, gu_1), (z_0, z_1))


def forward(hidden, weights, gains, tables):
    w_qkv, w_out, w_gu, w_down = weights
    after_mixer, saved = forward_mixer(hidden, w_qkv, w_out, gains, tables)
    out, saved_dense = forward_dense(after_mixer, w_gu, w_down, gains)
    return out, saved + saved_dense


def dense_back_kernel(first, *refs):
    sofar, refs = (None, refs) if first else (refs[0], refs[1:])
    dm, wd, gu, w, dgu_out, da2 = refs

    @pl.when(pl.program_id(0) == 0)
    def _():
        da2[...] = jnp.zeros_like(da2) if first else sofar[...]

    dz = dot_t(dm[...], wd[...])
    gate, up = gu[:, :512], gu[:, 512:]
    sig = jax.nn.sigmoid(gate)
    dg = (dz * up * sig * (1.0 + gate * (1.0 - sig))).astype(low)
    du = (dz * (gate * sig)).astype(low)
    dgu_out[:, :512] = dg
    dgu_out[:, 512:] = du
    da2[...] += dot_t(dgu_out[...], w[...])


def dense_back_half(half, sofar, dm, gu, w_half, w_down):
    ins = [] if half == 1 else [(whole(BLOCK), sofar)]
    ins += [(whole(BLOCK), dm), (rows_at(512, MODEL, 3 * half), w_down)]
    ins += [(columns_at(256, 1024), gu), (columns_at(MODEL, 1024), w_half)]
    outs = [(columns_at(256, 1024), shape_of(256, 3072, low)), (whole(BLOCK), shape_of(*BLOCK, f32))]
    kernel = functools.partial(dense_back_kernel, half == 1)
    return call(kernel, 3, ins, outs)


def normed_back(upstream, normed, scale, gain):
    gain_part = jnp.sum(upstream * normed, axis=0, keepdims=True)
    scaled = upstream * gain
    return scale * (scaled - normed * jnp.mean(scaled * normed, axis=-1, keepdims=True)), gain_part


def attention_back_kernel(first, *refs):
    sofar, refs = (None, refs) if first else (refs[:3], refs[3:])
    dr, wo, qkv, qg, kg, cosine, sine, w, dqkv_out, da1, q_grad, k_grad = refs

    @pl.when(pl.program_id(0) == 0)
    def _():
        for k, ref in enumerate((da1, q_grad, k_grad)):
            ref[...] = jnp.zeros_like(ref) if first else sofar[k][...]

    datt = dot_t(dr[...], wo[...]).astype(low)
    for s in range(2):
        rows = slice(128 * s, 128 * s + 128)
        cos, sin = cosine[...], sine[...]
        qr, kr, v, qn, kn, q_scale, k_scale = scaled_heads(qkv[rows, :], qg[...], kg[...], cos, sin)
        p = soft_scores(qr, kr)
        do = jnp.concatenate([datt[rows, :HEAD], datt[rows, HEAD:]])
        dp = dot_t(do, v)
        dv = dot_first(p.astype(low), do)
        ds = (p * (dp - jnp.sum(dp * p, axis=-1, keepdims=True))).astype(low)
        dqr, dkr = dot(ds, kr) * ROOT, dot_first(ds, qr) * ROOT
        cos_two, sin_two = jnp.concatenate([cos] * 2), jnp.concatenate([sin] * 2)
        dq, q_part = normed_back(turned(dqr, cos_two, -sin_two), qn, q_scale, qg[...])
        dk, k_part = normed_back(turned(dkr, cos, -sin), kn, k_scale, kg[...])
        q_grad[...] += q_part
        k_grad[...] += k_part
        dq = dq.astype(low)
        dqkv_out[rows, :HEAD] = dq[:128]
        dqkv_out[rows, HEAD : 2 * HEAD] = dq[128:]
        dqkv_out[rows, 2 * HEAD : 3 * HEAD] = dk.astype(low)
        dqkv_out[rows, 3 * HEAD :] = dv.astype(low)
    da1[...] += dot_t(dqkv_out[...], w[...])


def attention_back_half(half, sofar, dr, qkv, w_half, w_out, gains, tables, waits=()):
    head, table = whole((1, HEAD)), whole((128, HEAD))
    ins = [] if half == 1 else [(whole(BLOCK), sofar[0]), (head, sofar[1]), (head, sofar[2])]
    ins += [(whole(BLOCK), dr), (rows_at(256, MODEL, 4 * half), w_out), (columns_at(256, 512), qkv)]
    ins += [(head, gains[1][None]), (head, gains[2][None]), (table, tables[0]), (table, tables[1])]
    ins += [(columns_at(MODEL, 512), w_half)]
    outs = [(columns_at(256, 512), shape_of(256, 2048, low)), (whole(BLOCK), shape_of(*BLOCK, f32))]
    outs += [(head, shape_of(1, HEAD, f32))] * 2
    kernel = functools.partial(attention_back_kernel, half == 1)
    return call(kernel, 4, ins, outs, waits)


def backward(cotangent, saved, weights, gains, tables, between=None):
    w_qkv, w_out, w_gu, w_down = weights
    mixer_gain, query_gain, key_gain, dense_gain = gains
    hidden, a1, qkv, att, after_mixer, a2, gu, z = saved
    dm = cotangent.astype(low)
    dgu_1, da2 = dense_back_half(1, None, dm, gu[1], w_gu[1], w_down)
    dgu_0, da2 = dense_back_half(0, da2, dm, gu[0], w_gu[0], w_down)
    if between is not None:
        da2 = between[0]((dgu_0, dgu_1), da2)
    scale_two = row_scale(after_mixer)
    part, dense_gain_grad = norm_backward(da2, after_mixer * scale_two, scale_two, dense_gain)
    dh2 = cotangent + part
    dr = dh2.astype(low)
    g_out = None
    if between is not None:
        dr, g_out = between[1](dr)
    dqkv_1, *so_far = attention_back_half(1, None, dr, qkv[1], w_qkv[1], w_out, gains, tables)
    if between is not None:
        dr = between[3](dr, dqkv_1, g_out)
    dqkv_0, da1, q_grad, k_grad = attention_back_half(
        0, so_far, dr, qkv[0], w_qkv[0], w_out, gains, tables
    )
    if between is not None:
        da1 = between[2]((dqkv_0, dqkv_1), da1, g_out)
    scale_one = row_scale(hidden)
    part, mixer_gain_grad = norm_backward(da1, hidden * scale_one, scale_one, mixer_gain)
    dh = dh2 + part
    return dh, (mixer_gain_grad, dense_gain_grad, q_grad[0], k_grad[0])


def product(left, left_other, right, right_other):
    both_left = jnp.concatenate([left, left_other])
    both_right = jnp.concatenate([right, right_other])
    dims = (((0,), (0,)), ((), ()))
    return lax.dot_general(both_left, both_right, dims, preferred_element_type=f32).astype(low)


def on_device(
    boundary,
    mixer_gain,
    query_weight,
    key_weight,
    value_weight,
    output_weight,
    query_gain,
    key_gain,
    dense_gain,
    gate_weight,
    up_weight,
    down_weight,
):
    first_section = lax.axis_index("section") == 0
    x = lax.axis_index("dp")
    place_at = lax.axis_index("fsdp")
    core, y, z = place_at & 1, (place_at >> 1) & 3, place_at >> 3
    spot = (x, z, y)
    local = boundary[0, :, 0].astype(f32).reshape(256, MODEL)

    gain_tile = jnp.stack(
        [mixer_gain[0], dense_gain[0], jnp.pad(query_gain[0], (0, 56)), jnp.pad(key_gain[0], (0, 56))],
        axis=1,
    )
    gain_tile = jnp.pad(gain_tile, ((0, 0), (0, 124)))

    shards = (query_weight, key_weight, value_weight, output_weight)
    shards += (gate_weight, up_weight, down_weight)
    kept, sent = pack_halves([shard[0] for shard in shards], gain_tile, core)
    chip = in_order(kept, swap_core(sent), core, 0)
    zero = jnp.zeros_like(z)
    z_own = z ^ core

    with jax.named_scope("ag_dense"):
        d_0 = lax.dynamic_slice(chip, (x * 32, zero + 3200), (32, 4608))
        d_z = swap_z(d_0)
        d_pair = jnp.stack([d_0, d_z])
        d_near = near_y(d_pair)
        m_0 = chip[:, :3200]
        m_z = swap_z(m_0)
        d_near, m_z = tied(d_near, m_z)
        d_far = far_y(*d_near)
        m_pair = jnp.stack([m_0, m_z])
        d_far, m_pair = tied(d_far, m_pair)
        d_all = (jnp.concatenate([d_pair, d_near[0]]), jnp.concatenate([d_near[1], *d_far]))
        d_x = near_x(*d_all)
    with jax.named_scope("ag_mixer"):
        m_near = near_y(m_pair)
        m_far = far_y(*m_near)
        m_far, d_x = tied(m_far, d_x)
        moves, offsets = [], []
        spots = [(0, 0), (0, 1), (1, 0), (1, 1), (2, 0), (2, 1), (3, 0), (4, 0)]
        for (piece, index), (dz, dy) in zip(spots, origins):
            moves.append((piece, index, 0, 0, 128, 2176, 0))
            offsets.append(((z ^ dz) * 4 + ((y - dy) & 3)) * 128)
            block = ((z_own ^ dz) * 4 + ((y - dy) & 3)) * 256
            for k in range(2):
                for m in range(2):
                    moves.append((piece, index, 64 * k, 2176 + 512 * m, 64, 512, 1))
                    offsets.append(block + 128 * k + 64 * m)
        own_qkv, own_out = place(
            (m_pair, *m_near, *m_far), moves, offsets, ((MODEL, 2176), (2048, 512))
        )
        w_qkv = (own_qkv, swap_core(own_qkv))
        w_out = joined(own_out, core)
    tile = own_qkv[:, 2048:2052].astype(f32)
    gains = (
        tile[:, 0],
        tile[:, 2].reshape(16, 64)[:, :8].reshape(HEAD),
        tile[:, 3].reshape(16, 64)[:, :8].reshape(HEAD),
        tile[:, 1],
    )
    tables = rotation_tables(128)
    d_x_far = far_x(*d_x)

    def place_dense(part):
        moves, offsets = [], []
        for piece, dx in enumerate((0, 0, 1, 1, 3, 3, 2, 2)):
            turn = (x - dx) & 3
            for index, n in enumerate(range(4 * (piece & 1), 4 * (piece & 1) + 4)):
                dz, dy = origins[n]
                moves.append((piece, index, 0, 0, 32, 3072, 0))
                offsets.append(((z ^ dz) * 4 + ((y - dy) & 3)) * 128 + turn * 32)
                block = ((z_own ^ dz) * 4 + ((y - dy) & 3)) * 384 + (turn >> 1) * 192
                for m in range(3):
                    moves.append((piece, index, 0, 3072 + 512 * m, 32, 512, 1))
                    offsets.append(block + 64 * m + (turn & 1) * 32)
        return place((*d_all, *d_x, *d_x_far), moves, offsets, ((MODEL, 3072), (3072, 512)), (part, w_qkv[1]))

    own_dense = []

    def between_halves(part):
        own_dense.extend(place_dense(part))
        return (own_dense[0],)

    with jax.named_scope("f1"):
        early_mixer, _ = forward_mixer(local, w_qkv, w_out, gains, tables, between_halves)
    with jax.named_scope("ag_dense"):
        own_gu, own_down = own_dense
        w_gu = (own_gu, swap_core(own_gu))
        w_down = joined(own_down, core)
    weights = (w_qkv, w_out, w_gu, w_down)
    with jax.named_scope("f1"):
        early, _ = forward_dense(early_mixer, w_gu, w_down, gains)
    arrived = move_section(early.astype(low), 1).astype(f32)
    with jax.named_scope("f2"):
        out, saved = forward(jnp.where(first_section, local, arrived), weights, gains, tables)
    _, a1, _, att, _, a2, _, z_low = saved
    with jax.named_scope("b1"):
        early_dh, _ = backward(local, saved, weights, gains, tables)
    returned = move_section(early_dh.astype(low), -1).astype(f32)
    cotangent = jnp.where(first_section, returned, local)

    acts = jnp.concatenate([a1, att[1], att[0], a2, z_low[1], z_low[0]], axis=1)
    acts = swap_core(acts)
    a1_o, att_o = acts[:, :1024], (acts[:, 1024:2048], acts[:, 2048:3072])
    a2_o, z_o = acts[:, 3072:4096], (acts[:, 4096:5632], acts[:, 5632:])

    def by_halves(left, left_other, right, right_other):
        parts = [product(a, b, right, right_other) for a, b in zip(left, left_other)]
        return by_chip(jnp.concatenate(parts))

    cot_mine, cot_theirs = half_of(cotangent, core, 1), half_of(cotangent, 1 - core, 1)
    z_flip = z ^ core
    done = {}

    def after_dgu(dgu, da2):
        with jax.named_scope("g_gu"):
            g_gu = product(a2, a2_o, dgu[0], swap_core(dgu[1])).reshape(8, 128, 3072)
            da2, g_gu = tied(da2, g_gu)

            def columns_of(place, start=0, width=768):
                return lax.dynamic_slice_in_dim(g_gu, place * 768 + start, width, 2)

            done["gu"] = (columns_of, reduce_x_first(columns_of, x))
        with jax.named_scope("g_down"):
            dm_o = swap_core(cot_theirs.astype(low))
            g_down = by_halves(z_low, z_o, cot_mine.astype(low), dm_o)
            da2, g_down = tied(da2, g_down)
            done["down"] = g_down
        return da2

    def after_dr(dr):
        with jax.named_scope("g_out"):
            dr_o = swap_core(half_of(dr, 1 - core, 1))
            g_out = by_halves(att, att_o, half_of(dr, core, 1), dr_o)
            g_do = jnp.concatenate([done["down"], g_out], axis=2)
            dr, g_do = tied(dr, g_do)
        with jax.named_scope("rs_do"):
            done["do"] = reduce_y_first(g_do, z_flip, y)
        return dr, g_do

    def between_heads(dr, dqkv_1, g_do):
        first_x, first_y, dqkv_1 = tied(done["gu"][1], done["do"], dqkv_1)
        with jax.named_scope("g_qkv"):
            done["dqkv_o"] = swap_core(dqkv_1)
        ready = []
        with jax.named_scope("rs_gu"):
            ready.append(reduce_x_ready(done["gu"][0], x, first_x))
        with jax.named_scope("rs_do"):
            ready.append(reduce_y_ready(g_do, z_flip, y, first_y))
        dr, ready = tied(dr, ready)
        with jax.named_scope("rs_gu"):
            done["gu2"] = near_x_two(*ready[0])
        with jax.named_scope("rs_do"):
            done["do2"] = near_y_two(*ready[1])
        return dr

    def after_attention(dqkv, da1, g_do):
        own = dqkv[0]
        with jax.named_scope("g_qkv"):
            g_qkv = by_chip(product(a1, a1_o, own, done["dqkv_o"]))
            da1, g_qkv = tied(da1, g_qkv)
        with jax.named_scope("rs_q"):
            first = reduce_y_first(g_qkv, z, y)
        first, second = tied(first, done["do2"])
        with jax.named_scope("rs_q"):
            done["q"] = (g_qkv, reduce_y_second(g_qkv, z, y, first))
        with jax.named_scope("rs_gu"):
            mine = reduce_x_third(done["gu"][0], x, done["gu2"]).reshape(2, 4, 128, 768)
            done["g"] = (mine, reduce_y_first(mine, z, y))
        with jax.named_scope("rs_do"):
            done["s_do"] = added(*reduce_z(g_do, z_flip, y, second))
        return da1

    with jax.named_scope("b2"):
        dh, gain_grads = backward(
            cotangent, saved, weights, gains, tables, (after_dgu, after_dr, after_attention, between_heads)
        )
    endpoints = jnp.where(first_section, dh, out).reshape(1, 2, 1, 128, MODEL)
    g_qkv, q_second = done["q"]
    mine, g_first = done["g"]
    gain_part = jnp.concatenate(gain_grads).reshape(18, 128)
    mine, gain_part = tied(mine, gain_part)
    gain_part = summed_over(summed_x(gain_part), 1, 8)
    q_second, g_first = tied(q_second, g_first)
    with jax.named_scope("rs_gu"):
        g_second = reduce_y_second(mine, z, y, g_first)
    with jax.named_scope("rs_q"):
        q_z = reduce_z(g_qkv, z, y, q_second)
        q_z, g_second = tied(q_z, g_second)
        s_q = added(*q_z)
    with jax.named_scope("rs_gu"):
        s_gu = added(*reduce_z(mine, z, y, g_second))
    with jax.named_scope("rs_x"):
        s_do, s_qkv = quarters(done["s_do"][:384]), quarters(s_q)
        s_o = quarters(done["s_do"][384:])
        blocks = [s_qkv[:, :, k : k + 512] for k in range(0, 2048, 512)] + [s_do, s_o]
        mine = reduce_x(jnp.concatenate(blocks, axis=1), x)
        m_qkv = jnp.concatenate([mine[k : k + 32] for k in range(0, 128, 32)], axis=1)
        m_gu = jnp.concatenate([s_gu[k : k + 32] for k in range(0, 128, 32)], axis=1)
    with jax.named_scope("fin"):
        parts = (m_qkv, m_gu, mine[128:224], mine[224:])
        qkv, gu, down, out_w = finish(parts, x, core)

    def both(pair, start, width, block=None):
        block = block or pair[0].shape[1]

        def part(value):
            starts = range(start, value.shape[1], block)
            return jnp.concatenate([value[:, k : k + width] for k in starts], axis=1)

        return in_order(*(part(p) for p in pair), core, 1)[None]

    sums = summed_over(gain_part, 2, 4).reshape(-1)

    def gain_rows(start, width):
        return lax.dynamic_slice_in_dim(sums, start + place_at * width, width, 0)[None]

    return (
        endpoints,
        gain_rows(0, 64),
        both(qkv, 0, 256, 512),
        both(qkv, 256, 128, 512),
        both(qkv, 384, 128, 512),
        both(out_w, 0, 512),
        gain_rows(2048, 8),
        gain_rows(2176, 8),
        gain_rows(1024, 64),
        both(gu, 0, 512, 1024),
        both(gu, 512, 512, 1024),
        both(down, 0, 512),
    )


def solution(mesh):
    placed = (
        P("section", None, ("dp", "fsdp"), None, None),
        P("section", "fsdp"),
        P("section", "fsdp", None),
        P("section", "fsdp", None),
        P("section", "fsdp", None),
        P("section", "fsdp", None),
        P("section", "fsdp"),
        P("section", "fsdp"),
        P("section", "fsdp"),
        P("section", "fsdp", None),
        P("section", "fsdp", None),
        P("section", "fsdp", None),
    )
    return jax.shard_map(
        on_device,
        mesh=mesh,
        in_specs=placed,
        out_specs=(
            P("section", None, ("dp", "fsdp"), None, None),
            P("section", "fsdp"),
            P("section", "fsdp", None),
            P("section", "fsdp", None),
            P("section", "fsdp", None),
            P("section", "fsdp", None),
            P("section", "fsdp"),
            P("section", "fsdp"),
            P("section", "fsdp"),
            P("section", "fsdp", None),
            P("section", "fsdp", None),
            P("section", "fsdp", None),
        ),
        check_vma=False,
    )
```
